32 devices in a mesh: dom: 8 (over z, y), mat: 4 (over x, core).
Axes of the slice: x: 2, y: 2, z: 4, core: 2. Of those that a mesh axis runs over, the one named last changes fastest.
Arguments:
- orbitals: bfloat16 [2048, 12, 32, 128], P('dom', None, 'mat')
- potential: float32 [32, 32, 128], P('dom', 'mat'), may hold values from -3 to 3
- centre_first: int32 [2048], P('dom'), may hold values from 0 to 3
- centre_second: int32 [2048], P('dom'), may hold values from 0 to 31
- centre_third: int32 [2048], P('dom'), may hold values from 0 to 127
- correlation_pairs: int32 [16, 5, 2], P('dom'), may hold values from 0 to 1, as said below
Outputs:
- gram_rows: float32 [5, 256, 2048], P(None, 'mat', 'dom')
- hamiltonian_rows: float32 [5, 256, 2048], P(None, 'mat', 'dom')
The draws below stay inside these ranges and needn't reach their ends.
Inputs may be any that keep to these rules, and one draw needn't show every extreme that they name: correlation_pairs[g, k, b] refers to block b of the domain k - 2 away from block g's owner (wrapping); the pattern is symmetric between the two blocks, and every pair of blocks of one domain is 1.
All inputs are finite; a program needn't handle non-finite values.
Results may differ from the reference program's by a relative error of at most 0.00043.
Values may be sent and summed in bfloat16 or wider, within the bound.
No kernel may reach another device: no remote copies, remote signals or barrier semaphores. Data moves between devices by JAX's collectives and lax.ppermute only.
A program may use at most 128 MiB of HBM per device.

```python
import math
import jax
import jax.numpy as jnp
from jax import lax

ORB = 128
BLK_DEV = 2
CX = 4
CZ = 128
RAD = 6
NBLK = 16
ORBS = 2048
NX = 32
NY = 32
N_DOM = 8


def draw_orbitals(key, part):
    noise_key, shared_key = jax.random.split(key, 2)
    full_shape = (ORBS, 3 * CX, NY, CZ)
    rough_part = jax.random.normal(noise_key, full_shape, jnp.float32)
    shared = jax.random.normal(shared_key, (NBLK, 1, 3 * CX, NY, CZ), jnp.float32)
    shared = jnp.broadcast_to(shared, (NBLK, ORB, 3 * CX, NY, CZ)).reshape(full_shape)
    return (2.0 * (rough_part + 0.3 * shared) / math.sqrt(4.0 * RAD ** 3)).astype(jnp.bfloat16)


def draw_correlation_pairs(key, part):
    votes = jax.random.randint(key, (NBLK, 5, BLK_DEV), 0, 4)
    blocks = jnp.arange(NBLK, dtype=jnp.int32)
    owners = blocks // BLK_DEV
    member = blocks % BLK_DEV
    reach = jnp.arange(5, dtype=jnp.int32)
    column = jnp.arange(BLK_DEV, dtype=jnp.int32)
    domains = NBLK // BLK_DEV
    partner = jnp.mod(owners[:, None, None] + reach[None, :, None] - 2, domains) * BLK_DEV + column[None, None, :]
    mirror = votes[partner, (4 - reach)[None, :, None], member[:, None, None]]
    strongest = jnp.maximum(votes, mirror)
    needed = jnp.array([3, 2, 0, 2, 3], dtype=jnp.int32)[None, :, None]
    return (strongest >= needed).astype(jnp.int32)


def plant(values, key, low, top_value):
    place = [jax.random.randint(jax.random.fold_in(key, axis), (), 0, length) for axis, length in enumerate(values.shape)]
    widest = values.shape.index(max(values.shape))
    neighbour = place[:widest] + [(place[widest] + 1) % values.shape[widest]] + place[widest + 1:]
    return values.at[tuple(place)].set(low).at[tuple(neighbour)].set(top_value)


def steps_of(own_key, extent, shards, low, high):
    loudness = 1.0
    for position, parts in shards:
        heights = jax.random.uniform(jax.random.fold_in(jax.random.fold_in(own_key, 6), position), (parts,), jnp.float32, low / len(shards), high / len(shards))
        loudness = loudness * jnp.repeat(jnp.exp(heights), extent[position] // parts).reshape((-1,) + (1,) * (len(extent) - 1 - position))
    return loudness


def setup_inputs(seed: int = 0) -> dict:
    key_list = jax.random.split(jax.random.key(seed), 7)
    return {
        "orbitals": draw_orbitals(jax.random.fold_in(key_list[6], 71), 0),
        "potential": jnp.clip(jax.random.uniform(key_list[1], (NX, NY, CZ), jnp.float32, -3.0, 3.0) * steps_of(key_list[1], (NX, NY, CZ), ((0, 8), (1, 4)), -0.4, 0.0), -3.0, 3.0),
        "centre_first": plant(jax.random.randint(key_list[2], (ORBS,), 0, CX), jax.random.fold_in(key_list[2], 1), 0, CX - 1).astype(jnp.int32),
        "centre_second": plant(jax.random.randint(key_list[3], (ORBS,), 0, NY), jax.random.fold_in(key_list[3], 1), 0, NY - 1).astype(jnp.int32),
        "centre_third": plant(jax.random.randint(key_list[4], (ORBS,), 0, CZ), jax.random.fold_in(key_list[4], 1), 0, CZ - 1).astype(jnp.int32),
        "correlation_pairs": draw_correlation_pairs(jax.random.fold_in(key_list[6], 71), 0),
    }


def sphere_mask(centre_first, centre_second, centre_third, window_cells, patch_cells, second_cells, second_start, second_total, third_cells):
    planes = lax.iota(jnp.int32, window_cells)
    off_first = planes[None, :] - (patch_cells + centre_first[:, None])
    interior = (planes >= 1) & (planes <= window_cells - 2)
    second_coord = second_start + lax.iota(jnp.int32, second_cells)
    off_second = jnp.mod(second_coord[None, :] - centre_second[:, None], second_total)
    off_second = jnp.minimum(off_second, second_total - off_second)
    off_third = lax.iota(jnp.int32, third_cells)[None, :] - centre_third[:, None]
    radius = window_cells // 2
    distance = (off_first * off_first)[:, :, None, None] + (off_second * off_second)[:, None, :, None] + (off_third * off_third)[:, None, None, :]
    return (distance <= radius * radius) & interior[None, :, None, None]


def stencil(extended, potential_slab):
    centre_cells = extended[:, 1:-1, 1:-1, :].astype(jnp.float32)
    beside = extended[:, 2:, 1:-1, :].astype(jnp.float32) + extended[:, :-2, 1:-1, :].astype(jnp.float32)
    beside = beside + extended[:, 1:-1, 2:, :].astype(jnp.float32) + extended[:, 1:-1, :-2, :].astype(jnp.float32)
    third_padded = jnp.pad(centre_cells, ((0, 0), (0, 0), (0, 0), (1, 1)))
    beside = beside + third_padded[..., 2:] + third_padded[..., :-2]
    return 0.5 * (6.0 * centre_cells - beside) + potential_slab[None] * centre_cells


def reference(orbitals, potential, centre_first, centre_second, centre_third, correlation_pairs):
    block_orbs = BLK_DEV * ORB
    wrapped_potential = jnp.concatenate([potential[NX - CX:], potential, potential[:CX]], axis=0)

    def window_fields(owner_index):
        first_row = owner_index * block_orbs
        values = lax.dynamic_slice_in_dim(orbitals, first_row, block_orbs, 0)
        firsts = lax.dynamic_slice_in_dim(centre_first, first_row, block_orbs, 0)
        seconds = lax.dynamic_slice_in_dim(centre_second, first_row, block_orbs, 0)
        thirds = lax.dynamic_slice_in_dim(centre_third, first_row, block_orbs, 0)
        inside = sphere_mask(firsts, seconds, thirds, 3 * CX, CX, NY, 0, NY, CZ)
        masked = jnp.where(inside, values, jnp.zeros_like(values))
        padded = jnp.pad(masked, ((0, 0), (0, 0), (1, 1), (0, 0)), mode="wrap")
        padded = jnp.pad(padded, ((0, 0), (1, 1), (0, 0), (0, 0)))
        potential_window = lax.dynamic_slice_in_dim(wrapped_potential, owner_index * CX, 3 * CX, 0)
        applied = stencil(padded, potential_window).astype(jnp.bfloat16)
        return masked, applied

    def domain_terms(domain):
        orbital_parts = []
        applied_parts = []
        for slot_index in range(3):
            owner_index = jnp.mod(domain - 1 + slot_index, N_DOM).astype(jnp.int32)
            masked, applied = window_fields(owner_index)
            low_plane = (2 - slot_index) * CX
            orbital_parts.append(masked[:, low_plane:low_plane + CX])
            applied_parts.append(applied[:, low_plane:low_plane + CX])
        orbital_block = jnp.concatenate(orbital_parts, 0).reshape(3 * block_orbs, -1)
        applied_block = jnp.concatenate(applied_parts, 0).reshape(3 * block_orbs, -1)
        gram_full = lax.dot_general(orbital_block, orbital_block, (((1,), (1,)), ((), ())), preferred_element_type=jnp.float32)
        energy_full = lax.dot_general(applied_block, orbital_block, (((1,), (1,)), ((), ())), preferred_element_type=jnp.float32)
        return gram_full, energy_full

    gram_terms, energy_terms = lax.map(domain_terms, jnp.arange(N_DOM, dtype=jnp.int32))

    def assemble(partials):
        shaped = partials.reshape(N_DOM, 3, block_orbs, 3, block_orbs)
        assembled = jnp.zeros((N_DOM, 5, block_orbs, block_orbs), jnp.float32)
        for slot_index in range(3):
            strip_part = jnp.roll(shaped[:, :, :, slot_index, :], slot_index - 1, axis=0)
            assembled = assembled + jnp.pad(strip_part, ((0, 0), (2 - slot_index, slot_index), (0, 0), (0, 0)))
        return jnp.transpose(assembled, (1, 2, 0, 3)).reshape(5, block_orbs, ORBS)

    weights = correlation_pairs.astype(jnp.float32)
    column_weights = jnp.repeat(weights, ORB, axis=2)
    full_weights = jnp.repeat(column_weights, ORB, axis=0)
    select = jnp.transpose(full_weights, (1, 2, 0))
    return assemble(gram_terms) * select, assemble(energy_terms) * select
```

```python
import functools

import jax
import jax.numpy as jnp
from jax import lax
from jax.experimental import pallas as pl
from jax.experimental.pallas import tpu as pltpu
from jax.sharding import PartitionSpec as P

SKEW = 12
FOLD = 32
BF = jnp.bfloat16
F32 = jnp.float32


def row_gap(rows, centre, total):
    gap = jnp.abs(rows - centre)
    return jnp.minimum(gap, total - gap)


def pack_kernel(ids_ref, first_ref, second_ref, third_ref, x_ref, o_ref, scr, *, share, patch, total_rows):
    count, window, rows, cells = x_ref.shape
    radius = window // 2
    base = ids_ref[0] * share + pl.program_id(0) * count
    z = lax.broadcasted_iota(jnp.int32, (rows, cells), 1).astype(F32)
    y = (lax.broadcasted_iota(jnp.int32, (rows, cells), 0) + ids_ref[1] * rows).astype(F32)

    def body(n, carry):
        i = base + n
        first = first_ref[i]
        off_z = z - third_ref[i].astype(F32)
        off_y = row_gap(y, second_ref[i].astype(F32), float(total_rows))
        distance = off_z * off_z + off_y * off_y
        packed = jnp.zeros((rows, cells), F32)
        for p in range(1, window - 1):
            off = p - patch - first
            limit = (radius * radius - off * off).astype(F32)
            kept = jnp.where(distance <= limit, x_ref[n, p].astype(F32), 0.0)
            packed = packed + pltpu.roll(kept, (SKEW * p) % cells, 1)
        scr[n] = packed
        return carry

    lax.fori_loop(0, count, body, 0, unroll=4)
    for r in range(rows):
        o_ref[r] = scr[:, r, :].astype(BF)


def pack_share(orbitals, firsts, seconds, thirds, share_id, row_group, share, patch, total_rows):
    _, window, rows, cells = orbitals.shape
    step = 16
    steps = share // step
    grid_spec = pltpu.PrefetchScalarGridSpec(
        num_scalar_prefetch=4,
        grid=(steps,),
        in_specs=[pl.BlockSpec((step, window, rows, cells), lambda s, ids, *_: (ids[0] * steps + s, 0, 0, 0))],
        out_specs=pl.BlockSpec((rows, step, cells), lambda s, *_: (0, s, 0)),
        scratch_shapes=[pltpu.VMEM((step, rows, cells), F32)],
    )
    return pl.pallas_call(
        functools.partial(pack_kernel, share=share, patch=patch, total_rows=total_rows),
        grid_spec=grid_spec,
        out_shape=jax.ShapeDtypeStruct((rows, share, cells), BF),
        compiler_params=pltpu.CompilerParams(vmem_limit_bytes=32 * 2**20),
        cost_estimate=pl.CostEstimate(flops=share * window * rows * cells * 8, bytes_accessed=share * window * rows * cells * 2, transcendentals=0),
    )(jnp.stack([share_id, row_group]), firsts, seconds, thirds, orbitals)


def merge_kernel(ids_ref, own_ref, near_ref, far_ref, diag_ref, centre_ref, o_ref):
    rows, share, cells = own_ref.shape
    parity = ids_ref[0] % 2
    o_ref[pl.ds(parity * rows, rows)] = own_ref[...] + far_ref[...]
    o_ref[pl.ds((1 - parity) * rows, rows)] = near_ref[...] + diag_ref[...]
    centres = centre_ref[pl.ds(pl.multiple_of(ids_ref[0] * share, share), share), :]
    lane = lax.broadcasted_iota(jnp.int32, (share, cells), 1)
    meta = jnp.where(lane == 0, centres[:, 0:1], jnp.where(lane == 1, centres[:, 1:2], centres[:, 2:3]))
    o_ref[2 * rows] = meta.astype(BF)


def merge_rows(ids, own, near, far, diag, centres):
    rows, share, cells = own.shape
    return pl.pallas_call(
        merge_kernel,
        in_specs=[pl.BlockSpec(memory_space=pltpu.SMEM)] + [pl.BlockSpec(memory_space=pltpu.VMEM)] * 5,
        out_specs=pl.BlockSpec(memory_space=pltpu.VMEM),
        out_shape=jax.ShapeDtypeStruct((2 * rows + 1, share, cells), BF),
        compiler_params=pltpu.CompilerParams(vmem_limit_bytes=32 * 2**20),
    )(ids, own, near, far, diag, centres)


def product_kernel(
    ids_ref, pairs_ref, row_third_ref,
    own_ref, near_ref, far_ref, diag_ref, low2_ref, low1_ref, up1_ref, up2_ref,
    v_own_ref, v_low_ref, v_up_ref,
    gram_ref, ham_ref,
    a_ref, b_ref, t_ref, v_ref, g_ref,
    *, patch, radius, total_rows,
):
    m = ids_ref[0]
    slots = own_ref.shape[0] - 1
    share, cells = own_ref.shape[1:]
    window = 3 * patch
    groups, _, rows, _ = v_own_ref.shape
    lane = lax.broadcasted_iota(jnp.int32, (share, cells), 1)

    for d, ref in enumerate((v_low_ref, v_own_ref, v_up_ref)):
        for group in range(groups):
            piece = jnp.bitwise_xor(group, m)
            for p in range(patch):
                v_ref[d, p, group * rows : (group + 1) * rows, :] = pltpu.roll(ref[piece, p], (FOLD * p) % cells, 1) if p else ref[piece, p]

    def centre_columns(ref):
        meta = ref[slots].astype(F32)
        return [jnp.broadcast_to(meta[:, c : c + 1], (share, cells)) for c in range(3)]

    def unpack(ref, planes, store):
        first, second, third = centre_columns(ref)
        for p in planes:
            z = jnp.bitwise_and(lane - FOLD * (p % patch), cells - 1).astype(F32)
            off_z = z - third
            off = float(p - patch) - first
            t_ref[p] = (float(radius * radius) - off * off - off_z * off_z).astype(BF)

        def body(s, carry):
            gaps = []
            for half in range(total_rows // slots):
                y = (s + half * slots).astype(F32)
                gap = row_gap(jnp.full((share, cells), y, F32), second, float(total_rows))
                gaps.append((gap * gap).astype(BF))
            packed = ref[s]
            parts = [{} for _ in gaps]
            for p in planes:
                moved = pltpu.roll(packed, ((FOLD - SKEW) * p) % cells, 1)
                limit = t_ref[p]
                for half, gap in enumerate(gaps):
                    before = parts[half].get(p // patch)
                    if before is None:
                        before = jnp.zeros_like(moved)
                    parts[half][p // patch] = jnp.where(gap <= limit, moved, before)
            for half in range(len(gaps)):
                column = pl.ds(pl.multiple_of((s + half * slots) * cells, cells), cells)
                for q, value in parts[half].items():
                    store(q, column, value)
            return carry

        lax.fori_loop(0, slots, body, 0)

    every = range(1, window - 1)
    for hop, ref in ((0, own_ref), (2, far_ref), (1, near_ref), (3, diag_ref)):
        who = pl.multiple_of(jnp.bitwise_xor(m, hop) * share, share)

        def store_row(q, column, value, who=who):
            a_ref[q, pl.ds(who, share), column] = value

        unpack(ref, every, store_row)

    def stencil(k, ref, planes):
        d = k - 2
        quads = sorted({p // patch for p in planes})

        def place(q):
            return q + d, (2 - q) * 2 * share

        def store_column(q, column, value):
            iq, at = place(q)
            b_ref[iq, at : at + share, column] = value

        unpack(ref, planes, store_column)
        third = centre_columns(ref)[2]
        for p in range(patch):
            z = jnp.bitwise_and(lane - FOLD * p, cells - 1).astype(F32)
            g_ref[p] = (jnp.abs(z - third) <= float(FOLD // 2 - 1)).astype(F32)

        def body(y, carry):
            here = pl.ds(pl.multiple_of(y * cells, cells), cells)
            after = pl.ds(pl.multiple_of(jnp.bitwise_and(y + 1, total_rows - 1) * cells, cells), cells)
            before = pl.ds(pl.multiple_of(jnp.bitwise_and(y - 1, total_rows - 1) * cells, cells), cells)
            part = 16
            for c in range(0, share, part):
                mine = [g_ref[p, c : c + part, :] > 0.5 for p in range(patch)]
                centre, up, down = {}, {}, {}
                for q in quads:
                    iq, at = place(q)
                    centre[q] = b_ref[iq, at + c : at + c + part, here].astype(F32)
                    up[q] = pltpu.roll(centre[q], FOLD, 1)
                    down[q] = pltpu.roll(centre[q], cells - FOLD, 1)
                zero = jnp.zeros((part, cells), F32)
                for q in quads:
                    iq, at = place(q)
                    below = jnp.where(mine[0], up.get(q - 1, zero), up[q])
                    above = jnp.where(mine[patch - 1], down.get(q + 1, zero), down[q])
                    beside = above + below
                    beside = beside + b_ref[iq, at + c : at + c + part, after].astype(F32)
                    beside = beside + b_ref[iq, at + c : at + c + part, before].astype(F32)
                    beside = beside + pltpu.roll(centre[q], cells - 1, 1) + pltpu.roll(centre[q], 1, 1)
                    v = [v_ref[iq, p, pl.ds(y, 1), :] for p in range(patch)]
                    v = [jnp.broadcast_to(row, (part, cells)) for row in v]
                    field = v[patch - 1]
                    for p in range(patch - 1):
                        field = jnp.where(mine[p], v[p], field)
                    applied = 0.5 * (6.0 * centre[q] - beside) + field * centre[q]
                    b_ref[iq, at + share + c : at + share + c + part, here] = applied.astype(BF)
            return carry

        lax.fori_loop(0, total_rows, body, 0)

    stencil(2, own_ref, every)
    stencil(1, low1_ref, range(patch, window - 1))
    stencil(3, up1_ref, range(1, 2 * patch))
    stencil(0, low2_ref, range(2 * patch, window - 1))
    stencil(4, up2_ref, range(1, patch))

    sums = {}
    both = 2 * share
    for q in range(3):
        product = lax.dot_general(b_ref[q], a_ref[q], (((1,), (1,)), ((), ())), preferred_element_type=F32)
        for s in range(3):
            k = q + s
            piece = product[s * both : (s + 1) * both]
            sums[k] = piece if k not in sums else sums[k] + piece

    half_rows = a_ref.shape[1] // pairs_ref.shape[0]
    column_block = (m * share) // half_rows
    row_third = row_third_ref[...]
    row_block = lax.broadcasted_iota(jnp.int32, (1, a_ref.shape[1]), 1) // half_rows
    for k, ref in enumerate((low2_ref, low1_ref, own_ref, up1_ref, up2_ref)):
        column_third = ref[slots].astype(F32)[:, 2:3]
        near = jnp.abs(row_third - column_third) <= float(FOLD // 2)
        weight = jnp.zeros((1, a_ref.shape[1]), F32)
        for g in range(pairs_ref.shape[0]):
            weight = jnp.where(row_block == g, pairs_ref[g, k, column_block].astype(F32), weight)
        weight = jnp.where(near, weight, 0.0)
        gram_ref[k] = sums[k][:share] * weight
        ham_ref[k] = sums[k][share:] * weight


def product(ids, pairs, row_third, packs, fields, patch, radius, total_rows, orbs):
    slots, share, cells = packs[0].shape
    reach = 2 * 2 + 1
    long = total_rows * cells
    vm = pl.BlockSpec(memory_space=pltpu.VMEM)
    sm = pl.BlockSpec(memory_space=pltpu.SMEM)
    out = jax.ShapeDtypeStruct((reach, share, orbs), F32)
    return pl.pallas_call(
        functools.partial(product_kernel, patch=patch, radius=radius, total_rows=total_rows),
        in_specs=[sm, sm, vm] + [vm] * 11,
        out_specs=[vm, vm],
        out_shape=[out, out],
        scratch_shapes=[
            pltpu.VMEM((3, orbs, long), BF),
            pltpu.VMEM((3, 6 * share, long), BF),
            pltpu.VMEM((3 * patch, share, cells), BF),
            pltpu.VMEM((3, patch, total_rows, cells), F32),
            pltpu.VMEM((patch, share, cells), F32),
        ],
        compiler_params=pltpu.CompilerParams(vmem_limit_bytes=56 * 2**20),
    )(ids, pairs, row_third, *packs, *fields)


def hop(x, k):
    return lax.ppermute(x, "mat", [(i, i ^ k) for i in range(lax.axis_size("mat"))])


def along(x, distance):
    size = lax.axis_size("dom")
    return lax.ppermute(x, "dom", [((i - distance) % size, i) for i in range(size)])


def on_device(orbitals, potential, centre_first, centre_second, centre_third, correlation_pairs):
    orbs, window, rows, cells = orbitals.shape
    patch = potential.shape[0]
    parts = lax.axis_size("mat")
    share = orbs // parts
    total_rows = rows * parts
    m = lax.axis_index("mat")
    ids = m[None]

    field = jnp.stack([potential] + [hop(potential, k) for k in range(1, parts)])
    field_low, field_up = along(field, 1), along(field, -1)

    def pack(k):
        return pack_share(orbitals, centre_first, centre_second, centre_third, m ^ k, m, share, patch, total_rows)

    arrived = {k: hop(pack(k), k) for k in (3, 2, 1)}
    centres = jnp.stack([centre_first, centre_second, centre_third], axis=1).astype(F32)
    merged = merge_rows(ids, pack(0), arrived[1], arrived[2], arrived[3], centres)

    low2, low1, up1, up2 = (along(merged, d) for d in (2, 1, -1, -2))
    far = hop(merged, 2)
    near = hop(merged, 1)
    diag = hop(far, 1)
    return tuple(
        product(
            ids, correlation_pairs, centre_third.astype(F32)[None, :],
            (merged, near, far, diag, low2, low1, up1, up2),
            (field, field_low, field_up),
            patch, window // 2, total_rows, orbs,
        )
    )


def solution(mesh):
    return jax.shard_map(
        on_device,
        mesh=mesh,
        in_specs=(
            P("dom", None, "mat", None),
            P("dom", "mat", None),
            P("dom"),
            P("dom"),
            P("dom"),
            P("dom", None, None),
        ),
        out_specs=(P(None, "mat", "dom"), P(None, "mat", "dom")),
        check_vma=False,
    )
```

```python
import functools

import jax
import jax.numpy as jnp
from jax import lax
from jax.experimental import pallas as pl
from jax.experimental.pallas import tpu as pltpu
from jax.sharding import PartitionSpec as P

STEP = 29
SKEW = STEP + 64
NEAR = 14
BF = jnp.bfloat16
F32 = jnp.float32
I32 = jnp.int32


def iota(shape, axis):
    return lax.broadcasted_iota(I32, shape, axis)


def pack_kernel(ids_ref, first_ref, second_ref, third_ref, x_ref, *rest, patch, rows, total_rows):
    *o_refs, landed, arrived, kept, moves, limits, scr = rest
    parts = len(o_refs)
    share, cells = o_refs[0].shape[1:]
    count = scr.shape[0]
    window = 3 * patch
    pairs = window // 2
    radius = window // 2
    thirds = pairs // 2
    m = ids_ref[0]

    def start_of(j, c):
        return pl.multiple_of(jnp.bitwise_xor(m, parts - 1 - j) * share + c * count, count)

    steps = [(j, c) for j in range(parts) for c in range(share // count)]
    copies = []
    for n, (j, c) in enumerate(steps):
        copies.append(pltpu.make_async_copy(x_ref.at[pl.ds(start_of(j, c), count)], landed.at[n], arrived.at[n]))
        copies[-1].start()

    source, target = iota((2 * cells, 2 * cells), 0), iota((2 * cells, 2 * cells), 1)
    to = jnp.bitwise_and(source + SKEW * (source // cells * pairs + target // cells), cells - 1)
    moves[...] = (to == jnp.bitwise_and(target, cells - 1)).astype(F32).astype(BF)
    plane = iota((2 * rows, cells), 0) // rows
    for a in range(pairs):
        p = plane + 2 * a
        inside = (p >= 1) & (p <= window - 2)
        for first in range(patch):
            off = p - patch - first
            limits[first, a] = jnp.where(inside, radius * radius - off * off, -1).astype(F32).astype(BF)
    z = iota((rows, cells), 1).astype(F32)
    y = (iota((rows, cells), 0) + m * rows).astype(F32)

    for step, (j, c) in enumerate(steps):
        base = start_of(j, c)
        copies[step].wait()

        def body(n, carry, base=base, step=step):
            i = base + n
            first = first_ref[i]
            off_z = z - third_ref[i].astype(F32)
            off_y = jnp.abs(y - second_ref[i].astype(F32))
            off_y = jnp.minimum(off_y, float(total_rows) - off_y)
            distance = off_z * off_z + off_y * off_y
            distance = jnp.concatenate([distance, distance], axis=0).astype(BF)
            at = pl.ds(pl.multiple_of(n * 2 * rows, 2 * rows), 2 * rows)
            for half in range(2):
                total = None
                for a in range(half * thirds, (half + 1) * thirds):
                    x = landed[step, n, 2 * a * rows : 2 * (a + 1) * rows, :]
                    x = jnp.where(distance <= limits[first, a], x, jnp.zeros_like(x))
                    turn = 2 * SKEW * (a - half * thirds) % cells
                    total = x if total is None else total + pltpu.roll(x, turn, 1)
                kept[at, half * cells : (half + 1) * cells] = total
            return carry

        lax.fori_loop(0, count, body, 0, unroll=8)
        moved = jnp.dot(kept[...], moves[...], preferred_element_type=F32).reshape(count, 2 * rows, 2 * cells)
        scr[...] = moved[:, :rows, :cells] + moved[:, rows:, cells:]
        for r in range(rows):
            o_refs[j][r, c * count : (c + 1) * count, :] = scr[:, r, :].astype(BF)


def pack(ids, firsts, seconds, thirds, orbitals, parts, patch):
    orbs, window, rows, cells = orbitals.shape
    share = orbs // parts
    count = share // 2
    steps = orbs // count
    sm = pl.BlockSpec(memory_space=pltpu.SMEM)
    return pl.pallas_call(
        functools.partial(pack_kernel, patch=patch, rows=rows, total_rows=rows * parts),
        in_specs=[sm] * 4 + [pl.BlockSpec(memory_space=pl.ANY)],
        out_specs=[pl.BlockSpec(memory_space=pltpu.VMEM)] * parts,
        out_shape=[jax.ShapeDtypeStruct((rows, share, cells), BF)] * parts,
        scratch_shapes=[
            pltpu.VMEM((steps, count, window * rows, cells), BF),
            pltpu.SemaphoreType.DMA((steps,)),
            pltpu.VMEM((count * 2 * rows, 2 * cells), BF),
            pltpu.VMEM((2 * cells, 2 * cells), BF),
            pltpu.VMEM((patch, window // 2, 2 * rows, cells), BF),
            pltpu.VMEM((count, rows, cells), F32),
        ],
        compiler_params=pltpu.CompilerParams(vmem_limit_bytes=58 * 2**20),
        cost_estimate=pl.CostEstimate(flops=orbitals.size * 128, bytes_accessed=orbitals.size * 2, transcendentals=0),
    )(ids, firsts, seconds, thirds, orbitals.reshape(orbs, window * rows, cells))


def merge_kernel(ids_ref, own_ref, near_ref, far_ref, diag_ref, centre_ref, *rest, patch):
    *field_refs, o_ref, v_ref = rest
    rows, share, cells = own_ref.shape
    m = ids_ref[0]
    parity = m % 2
    o_ref[pl.ds(parity * rows, rows)] = own_ref[...] + far_ref[...]
    o_ref[pl.ds((1 - parity) * rows, rows)] = near_ref[...] + diag_ref[...]
    centres = centre_ref[pl.ds(pl.multiple_of(m * share, share), share), :]
    lane = iota((share, cells), 1)
    meta = jnp.where(lane == 0, centres[:, 0:1], jnp.where(lane == 1, centres[:, 1:2], centres[:, 2:3]))
    o_ref[2 * rows] = meta.astype(BF)
    for hop, ref in enumerate(field_refs):
        at = pl.ds(pl.multiple_of(jnp.bitwise_xor(m, hop) * rows, rows), rows)
        for p in range(3 * patch):
            v_ref[p, at, :] = pltpu.roll(ref[p], STEP * p % cells, 1) if p else ref[p]


def merge_rows(ids, packs, centres, fields):
    rows, share, cells = packs[0].shape
    window = fields[0].shape[0]
    return pl.pallas_call(
        functools.partial(merge_kernel, patch=window // 3),
        in_specs=[pl.BlockSpec(memory_space=pltpu.SMEM)] + [pl.BlockSpec(memory_space=pltpu.VMEM)] * (5 + len(fields)),
        out_specs=[pl.BlockSpec(memory_space=pltpu.VMEM)] * 2,
        out_shape=[
            jax.ShapeDtypeStruct((2 * rows + 1, share, cells), BF),
            jax.ShapeDtypeStruct((window, rows * len(fields), cells), F32),
        ],
        compiler_params=pltpu.CompilerParams(vmem_limit_bytes=16 * 2**20),
    )(ids, *packs, centres, *fields)


class Source:
    def __init__(self, ref, hop, patch, total_rows):
        self.ref, self.hop, self.patch, self.total_rows = ref, hop, patch, total_rows
        self.slots = ref.shape[0] - 1
        self.share, self.cells = ref.shape[1:]
        meta = ref[self.slots].astype(F32)
        shape = (self.share, self.cells)
        self.first, self.second, self.third = (jnp.broadcast_to(meta[:, c : c + 1], shape) for c in range(3))
        self.start = iota(shape, 1) - self.third.astype(I32) + self.cells // 2
        self.row = self.second.astype(I32)

    def off(self, p):
        place = STEP * (p + self.patch * self.hop)
        return (jnp.bitwise_and(self.start - place, self.cells - 1) - self.cells // 2).astype(F32)

    def limit(self, p):
        off_z, off_x = self.off(p), float(p - self.patch) - self.first
        radius = 3 * self.patch // 2
        return float(radius * radius) - off_x * off_x - off_z * off_z

    def limits(self, plane_sets, out_ref):
        every = {p: self.limit(p) for p in sorted(set().union(*plane_sets))}
        for n, planes in enumerate(plane_sets):
            for odd in range(2):
                value = jnp.full((self.share, self.cells), -1.0, F32)
                for p in planes:
                    if p % 2 == odd:
                        value = jnp.maximum(value, every[p])
                out_ref[n, odd] = value.astype(BF)

    def gap(self, s):
        ahead = s - self.row
        off = jnp.bitwise_and(ahead + self.slots // 2, self.slots - 1) - self.slots // 2
        low = jnp.bitwise_and(ahead + self.slots // 2, self.total_rows - 1) < self.slots
        off = off.astype(F32)
        return (off * off).astype(BF), low.astype(F32)

    def packed(self, s):
        value = self.ref[s]
        turn = STEP * self.patch * self.hop
        even = pltpu.roll(value, turn % self.cells, 1) if turn % self.cells else value
        return even, pltpu.roll(value, (turn + self.cells // 2) % self.cells, 1)


def inside(gap, limit_ref, n, even, odd):
    zero = jnp.zeros_like(even)
    return jnp.where(gap <= limit_ref[n, 0], even, jnp.where(gap <= limit_ref[n, 1], odd, zero))


def planes_of(quads, allowed, patch, shift):
    return [[p for p in range(patch * q + shift, patch * (q + 1) + shift) if p in allowed] for q in quads]


def spread_rows(source, limit_ref, quads, store):
    def body(s, carry):
        even, odd = source.packed(s)
        gap, low = source.gap(s)
        is_low = low.astype(BF) > 0.5
        zero = jnp.zeros_like(even)
        for n, q in enumerate(quads):
            value = inside(gap, limit_ref, n, even, odd)
            store(q, s, jnp.where(is_low, value, zero))
            store(q, s + source.slots, jnp.where(is_low, zero, value))
        return carry

    lax.fori_loop(0, source.slots, body, 0, unroll=4)


def stencil_moves(cells):
    source, target = iota((2 * cells, 2 * cells), 0), iota((2 * cells, 2 * cells), 1)
    ahead = jnp.bitwise_and(target - source, cells - 1)
    same = source // cells == target // cells
    beside = (same & ((ahead == 1) | (ahead == cells - 1))) | (~same & (ahead == 0))
    value = jnp.where(same & (ahead == 0), 3.0, 0.0)
    return jnp.where(beside, -0.5, value).astype(F32).astype(BF)


def columns(source, allowed, limit_ref, group_ref, value_ref, plane_ref, moves_ref, v_ref, kinetic_ref, store):
    patch, cells, share, slots = source.patch, source.cells, source.share, source.slots
    shift = -patch * source.hop
    quads = sorted({(p - shift) // patch for p in allowed})
    sets = planes_of(quads, allowed, patch, shift) + planes_of(quads, allowed, patch, shift - 1) + planes_of(quads, allowed, patch, shift + 1)
    source.limits(sets, limit_ref)
    count = len(quads)
    for n, q in enumerate(quads):
        group = jnp.zeros((share, cells), F32)
        for g in range(1, patch):
            group = jnp.where(jnp.abs(source.off(patch * q + shift + g)) <= float(NEAR), float(g), group)
        group_ref[n] = group

    def place(n, pair):
        return pl.ds(pl.multiple_of((n * (slots // 2) + pair) * share, share), share)

    def first_pass(pair, carry):
        for half in range(2):
            s = 2 * pair + half
            even, odd = source.packed(s)
            gap, _ = source.gap(s)
            for n in range(count):
                at = place(n, pair)
                value_ref[at, half * cells : (half + 1) * cells] = inside(gap, limit_ref, n, even, odd)
                before = inside(gap, limit_ref, count + n, even, odd)
                plane_ref[at, half * cells : (half + 1) * cells] = pltpu.roll(before, STEP, 1)
                after = inside(gap, limit_ref, 2 * count + n, even, odd)
                plane_ref[at, (2 + half) * cells : (3 + half) * cells] = pltpu.roll(after, cells - STEP, 1)
        return carry

    lax.fori_loop(0, slots // 2, first_pass, 0, unroll=4)
    total = count * slots // 2 * share
    kinetic_ref[:total] = jnp.dot(value_ref[:total], moves_ref[...], preferred_element_type=F32)

    def second_pass(pair, carry):
        for half in range(2):
            s = 2 * pair + half
            _, low = source.gap(s)
            low_wide = low > 0.5
            low_packed = low.astype(BF) > 0.5
            neighbour = jnp.bitwise_and(pair + 2 * half - 1, slots // 2 - 1)
            here = slice(half * cells, (half + 1) * cells)
            there = slice((1 - half) * cells, (2 - half) * cells)
            for n, q in enumerate(quads):
                at = place(n, pair)
                value = value_ref[at, here]
                group = group_ref[n]
                field = None
                for g in range(patch):
                    rows = [v_ref[patch * q + g, pl.ds(y, 1), :] for y in (s, s + slots)]
                    row = jnp.where(low_wide, *rows)
                    field = row if g == 0 else jnp.where(group == float(g), row, field)
                beside = plane_ref[at, here].astype(F32) + plane_ref[at, slice((2 + half) * cells, (3 + half) * cells)].astype(F32)
                beside = beside + value_ref[place(n, neighbour), there].astype(F32)
                applied = kinetic_ref[at, here] - 0.5 * beside + field * value.astype(F32)
                applied = applied.astype(BF)
                zero = jnp.zeros_like(value)
                store(q, 0, s, jnp.where(low_packed, value, zero))
                store(q, 0, s + slots, jnp.where(low_packed, zero, value))
                store(q, 1, s, jnp.where(low_packed, applied, zero))
                store(q, 1, s + slots, jnp.where(low_packed, zero, applied))
        return carry

    lax.fori_loop(0, slots // 2, second_pass, 0, unroll=2)


def row_of(y, cells):
    return pl.ds(pl.multiple_of(y * cells, cells), cells)


def product_of(b, a):
    return lax.dot_general(b, a, (((1,), (1,)), ((), ())), preferred_element_type=F32)


def own_kernel(own_ref, v_ref, b_ref, limit_ref, group_ref, value_ref, plane_ref, moves_ref, kinetic_ref, *, patch, total_rows):
    share, cells = own_ref.shape[1:]
    moves_ref[...] = stencil_moves(cells)

    def store_column(q, applied, y, value):
        b_ref[q, applied * share : (applied + 1) * share, row_of(y, cells)] = value

    source = Source(own_ref, 0, patch, total_rows)
    every = range(1, 3 * patch - 1)
    columns(source, every, limit_ref, group_ref, value_ref, plane_ref, moves_ref, v_ref, kinetic_ref, store_column)


def rows_kernel(ids_ref, own_ref, near_ref, far_ref, diag_ref, b_ref, a_ref, sum_ref, limit_ref, *, patch, total_rows):
    m = ids_ref[0]
    share, cells = own_ref.shape[1:]
    every = range(1, 3 * patch - 1)
    for hop, ref in enumerate((own_ref, near_ref, far_ref, diag_ref)):
        who = pl.ds(pl.multiple_of(jnp.bitwise_xor(m, hop) * share, share), share)
        source = Source(ref, 0, patch, total_rows)
        source.limits(planes_of(range(3), every, patch, 0), limit_ref)

        def store_row(q, y, value, who=who):
            a_ref[q, who, row_of(y, cells)] = value

        spread_rows(source, limit_ref, range(3), store_row)
    total = product_of(b_ref[0], a_ref[0])
    for q in range(1, 3):
        total = total + product_of(b_ref[q], a_ref[q])
    sum_ref[...] = total


def others_kernel(
    ids_ref, pairs_ref, row_third_ref, own_ref, low2_ref, low1_ref, up1_ref, up2_ref, a_ref, v_ref, sum_ref,
    gram_ref, ham_ref,
    b_ref, limit_ref, group_ref, value_ref, plane_ref, moves_ref, kinetic_ref,
    *, patch, total_rows,
):
    m = ids_ref[0]
    slots = own_ref.shape[0] - 1
    share, cells = own_ref.shape[1:]
    both = 2 * share
    window = 3 * patch
    moves_ref[...] = stencil_moves(cells)
    spots = {}
    for hop, ref, allowed in (
        (-1, low1_ref, range(patch, window - 1)),
        (1, up1_ref, range(1, 2 * patch)),
        (-2, low2_ref, range(2 * patch, window - 1)),
        (2, up2_ref, range(1, patch)),
    ):
        def store_column(q, applied, y, value, hop=hop):
            taken = sorted({q - 2, q - 1, q} - {0}).index(hop)
            spots[hop, q] = taken
            at = taken * both + applied * share
            b_ref[q, at : at + share, row_of(y, cells)] = value

        source = Source(ref, hop, patch, total_rows)
        columns(source, allowed, limit_ref, group_ref, value_ref, plane_ref, moves_ref, v_ref, kinetic_ref, store_column)

    sums = {0: sum_ref[...]}
    for q in range(3):
        product = product_of(b_ref[q], a_ref[q])
        for (hop, at_q), taken in spots.items():
            if at_q == q:
                piece = product[taken * both : (taken + 1) * both]
                sums[hop] = piece if hop not in sums else sums[hop] + piece

    orbs = a_ref.shape[1]
    half_rows = orbs // pairs_ref.shape[0]
    column_block = (m * share) // half_rows
    row_third = row_third_ref[...]
    row_block = iota((1, orbs), 1) // half_rows
    for k, ref in enumerate((low2_ref, low1_ref, own_ref, up1_ref, up2_ref)):
        column_third = ref[slots].astype(F32)[:, 2:3]
        weight = jnp.zeros((1, orbs), F32)
        for g in range(pairs_ref.shape[0]):
            weight = jnp.where(row_block == g, pairs_ref[g, k, column_block].astype(F32), weight)
        weight = jnp.where(jnp.abs(row_third - column_third) <= float(NEAR), weight, 0.0)
        gram_ref[k] = sums[k - 2][:share] * weight
        ham_ref[k] = sums[k - 2][share:] * weight


def products(ids, pairs, row_third, rows, others, v, total_rows, orbs):
    slots, share, cells = rows[0].shape
    patch = v.shape[0] // 3
    slots -= 1
    long = total_rows * cells
    vm = pl.BlockSpec(memory_space=pltpu.VMEM)
    sm = pl.BlockSpec(memory_space=pltpu.SMEM)
    params = pltpu.CompilerParams(vmem_limit_bytes=26 * 2**20)
    cost = pl.CostEstimate(flops=3 * 10**9, bytes_accessed=10 * 10**6, transcendentals=0)
    sizes = dict(patch=patch, total_rows=total_rows)

    def scratch(quads):
        tall = quads * slots // 2 * share
        return [
            pltpu.VMEM((3 * quads, 2, share, cells), BF),
            pltpu.VMEM((quads, share, cells), F32),
            pltpu.VMEM((tall, 2 * cells), BF),
            pltpu.VMEM((tall, 4 * cells), BF),
            pltpu.VMEM((2 * cells, 2 * cells), BF),
            pltpu.VMEM((tall, 2 * cells), F32),
        ]

    b = pl.pallas_call(
        functools.partial(own_kernel, **sizes),
        in_specs=[vm] * 2,
        out_specs=vm,
        out_shape=jax.ShapeDtypeStruct((3, 2 * share, long), BF),
        scratch_shapes=scratch(3),
        compiler_params=params,
        cost_estimate=cost,
    )(rows[0], v)
    a, own_sum = pl.pallas_call(
        functools.partial(rows_kernel, **sizes),
        in_specs=[sm] + [vm] * 5,
        out_specs=[vm] * 2,
        out_shape=[jax.ShapeDtypeStruct((3, orbs, long), BF), jax.ShapeDtypeStruct((2 * share, orbs), F32)],
        scratch_shapes=[pltpu.VMEM((3, 2, share, cells), BF)],
        compiler_params=params,
        cost_estimate=cost,
    )(ids, *rows, b)
    out = jax.ShapeDtypeStruct((5, share, orbs), F32)
    return pl.pallas_call(
        functools.partial(others_kernel, **sizes),
        in_specs=[sm, sm] + [vm] * 9,
        out_specs=[vm, vm],
        out_shape=[out, out],
        scratch_shapes=[pltpu.VMEM((3, 4 * share, long), BF)] + scratch(2),
        compiler_params=params,
        cost_estimate=cost,
    )(ids, pairs, row_third, rows[0], *others, a, v, own_sum)


def hop(x, k):
    return lax.ppermute(x, "mat", [(i, i ^ k) for i in range(lax.axis_size("mat"))])


def along(x, distance):
    size = lax.axis_size("dom")
    return lax.ppermute(x, "dom", [((i - distance) % size, i) for i in range(size)])


def on_device(orbitals, potential, centre_first, centre_second, centre_third, correlation_pairs):
    orbs, window, rows, cells = orbitals.shape
    patch = potential.shape[0]
    parts = lax.axis_size("mat")
    ids = lax.axis_index("mat")[None]

    field = jnp.concatenate([along(potential, 1), potential, along(potential, -1)], axis=0)
    fields = [field] + [hop(field, k) for k in range(1, parts)]

    diag, far, near, own = pack(ids, centre_first, centre_second, centre_third, orbitals, parts, patch)
    centres = jnp.stack([centre_first, centre_second, centre_third], axis=1).astype(F32)
    merged, v = merge_rows(ids, (own, hop(near, 1), hop(far, 2), hop(diag, 3)), centres, fields)

    others = [along(merged, d) for d in (2, 1, -1, -2)]
    far = hop(merged, 2)
    near = hop(merged, 1)
    diag = hop(far, 1)
    row_third = centre_third.astype(F32)[None, :]
    return tuple(products(ids, correlation_pairs, row_third, (merged, near, far, diag), others, v, rows * parts, orbs))


def solution(mesh):
    return jax.shard_map(
        on_device,
        mesh=mesh,
        in_specs=(
            P("dom", None, "mat", None),
            P("dom", "mat", None),
            P("dom"),
            P("dom"),
            P("dom"),
            P("dom", None, None),
        ),
        out_specs=(P(None, "mat", "dom"), P(None, "mat", "dom")),
        check_vma=False,
    )
```

```python
import functools

import jax
import jax.numpy as jnp
from jax import lax
from jax.experimental import pallas as pl
from jax.experimental.pallas import tpu as pltpu
from jax.sharding import PartitionSpec as P

STEP = 29
SKEW = STEP + 64
NEAR = 14
PAIR_SKEW, PAIR_ROW = 22, 32
P_STEP, P_UNROLL = 16, 1
A_PART, A_STEP, A_UNROLL = 16, 8, 1
S_PART, S_UNROLL = 32, 16
BF = jnp.bfloat16
F32 = jnp.float32
I32 = jnp.int32


def iota(shape, axis):
    return lax.broadcasted_iota(I32, shape, axis)


def half_of(m, own):
    return jnp.bitwise_xor(m // 2, 1 - own)


def pack_kernel(ids_ref, centre_in, x_ref, *rest, patch, rows, total_rows):
    *o_refs, landed, arrived, limits, scr, centre_ref, told = rest
    _, half, cells = o_refs[0].shape
    steps, count = landed.shape[:2]
    window = 3 * patch
    pairs = window // 2
    radius = window // 2
    m = ids_ref[0]

    def start_of(step):
        return pl.multiple_of(half_of(m, step * count // half) * half + step * count % half, count)

    copies = []
    for step in range(steps):
        copies.append(pltpu.make_async_copy(x_ref.at[pl.ds(start_of(step), count)], landed.at[step], arrived.at[step]))
        copies[-1].start()
    centre_copy = pltpu.make_async_copy(centre_in, centre_ref, told.at[0])
    centre_copy.start()

    plane = iota((2 * rows, cells), 0) // rows
    for a in range(pairs):
        p = plane + 2 * a
        inside = (p >= 1) & (p <= window - 2)
        for first in range(patch):
            off = p - patch - first
            limits[first, a] = jnp.where(inside, radius * radius - off * off, -1).astype(F32).astype(BF)
    z = iota((rows, cells), 1).astype(F32)
    y = (iota((rows, cells), 0) + m * rows).astype(F32)

    centre_copy.wait()
    for step in range(steps):
        copies[step].wait()

        def body(n, carry, base=start_of(step), step=step):
            found = []
            for i in range(P_STEP):
                at = n * P_STEP + i
                first = centre_ref[0, base + at]
                off_z = z - centre_ref[2, base + at].astype(F32)
                off_y = jnp.abs(y - centre_ref[1, base + at].astype(F32))
                off_y = jnp.minimum(off_y, float(total_rows) - off_y)
                distance = off_z * off_z + off_y * off_y
                distance = jnp.concatenate([distance, distance], axis=0).astype(BF)
                total = None
                for a in range(pairs):
                    x = landed[step, at, 2 * a * rows : 2 * (a + 1) * rows, :]
                    x = jnp.where(distance <= limits[first, a], x, jnp.zeros_like(x))
                    turn = 2 * SKEW * a % cells
                    total = x if total is None else total + pltpu.roll(x, turn, 1)
                odd = pltpu.roll(total, SKEW, 1)
                found.append((at, total.astype(F32)[:rows] + odd.astype(F32)[rows:]))
            for at, value in found:
                scr[at] = value
            return carry

        lax.fori_loop(0, count // P_STEP, body, 0, unroll=P_UNROLL)
        for r in range(rows):
            at = step * count % half
            o_refs[step * count // half][r, at : at + count, :] = scr[:, r, :].astype(BF)


def pack(ids, centres, orbitals, parts, patch):
    orbs, window, rows, cells = orbitals.shape
    steps = 8
    count = orbs // steps
    sm = pl.BlockSpec(memory_space=pltpu.SMEM)
    return pl.pallas_call(
        functools.partial(pack_kernel, patch=patch, rows=rows, total_rows=rows * parts),
        in_specs=[sm] + [pl.BlockSpec(memory_space=pl.ANY)] * 2,
        out_specs=[pl.BlockSpec(memory_space=pltpu.VMEM)] * 2,
        out_shape=[jax.ShapeDtypeStruct((rows, orbs // 2, cells), BF)] * 2,
        scratch_shapes=[
            pltpu.VMEM((steps, count, window * rows, cells), BF),
            pltpu.SemaphoreType.DMA((steps,)),
            pltpu.VMEM((patch, window // 2, 2 * rows, cells), BF),
            pltpu.VMEM((count, rows, cells), F32),
            pltpu.SMEM(centres.shape, I32),
            pltpu.SemaphoreType.DMA((1,)),
        ],
        compiler_params=pltpu.CompilerParams(vmem_limit_bytes=53 * 2**20),
        cost_estimate=pl.CostEstimate(flops=orbitals.size * 256, bytes_accessed=orbitals.size * 2, transcendentals=0),
    )(ids, centres, orbitals.reshape(orbs, window * rows, cells))


def merge_kernel(ids_ref, centre_ref, *refs, chips, own_only, patch):
    m = ids_ref[0]
    parity = m % 2
    o_refs = refs[4 * chips :]
    share = o_refs[0].shape[1]
    for chip in range(chips):
        own_ref, near_ref, far_ref, diag_ref = refs[4 * chip : 4 * chip + 4]
        rows, half, cells = own_ref.shape
        for n in [None] if own_only else range(half // share):
            o_ref = o_refs[0] if own_only else o_refs[chip * half // share + n]
            start = parity * share if own_only else n * share
            source = pl.ds(pl.multiple_of(start, share), share)
            centres = centre_ref[pl.ds(pl.multiple_of(half_of(m, 1 - chip) * half + start, share), share), :]
            lane = iota((share, cells), 1)
            meta = jnp.where(lane == 0, centres[:, 0:1], jnp.where(lane == 1, centres[:, 1:2], centres[:, 2:3]))
            o_ref[pl.ds(parity * rows, rows)] = own_ref[:, source, :] + far_ref[:, source, :]
            o_ref[pl.ds((1 - parity) * rows, rows)] = near_ref[:, source, :] + diag_ref[:, source, :]
            o_ref[2 * rows] = meta.astype(BF)
    if own_only:
        o_ref, low_ref, up_ref, gap_ref = o_refs
        source = Source(o_ref, 0, patch, 4 * rows, SKEW)
        source.gaps(gap_ref)
        tighten(source, gap_ref, range(2 * patch, 3 * patch - 1), low_ref)
        tighten(source, gap_ref, range(1, patch), up_ref)


def merge_rows(ids, centres, share, patch, own_only, *packs):
    rows, half, cells = packs[0][0].shape
    units = [2 * rows + 1, rows // 2 + 1, rows // 2 + 1] if own_only else [2 * rows + 1] * (len(packs) * half // share)
    return pl.pallas_call(
        functools.partial(merge_kernel, chips=len(packs), own_only=own_only, patch=patch),
        in_specs=[pl.BlockSpec(memory_space=pltpu.SMEM)] + [pl.BlockSpec(memory_space=pltpu.VMEM)] * (1 + 4 * len(packs)),
        out_specs=[pl.BlockSpec(memory_space=pltpu.VMEM)] * len(units),
        out_shape=[jax.ShapeDtypeStruct((n, share, cells), BF) for n in units],
        scratch_shapes=[pltpu.VMEM((2, 2 * rows, share, cells), BF)] if own_only else [],
        compiler_params=pltpu.CompilerParams(vmem_limit_bytes=16 * 2**20),
    )(ids, centres, *(array for pack in packs for array in pack))


class Source:
    def __init__(self, ref, hop, patch, total_rows, step=STEP):
        self.ref, self.hop, self.patch, self.total_rows, self.step = ref, hop, patch, total_rows, step
        self.slots = total_rows // 2
        units, self.share, self.cells = ref.shape
        meta = ref[units - 1].astype(F32)
        shape = (self.share, self.cells)
        self.first, self.second, self.third = (jnp.broadcast_to(meta[:, c : c + 1], shape) for c in range(3))
        self.start = iota(shape, 1) - self.third.astype(I32) + self.cells // 2

    def off(self, p):
        place = self.step * (p + self.patch * self.hop)
        return (jnp.bitwise_and(self.start - place, self.cells - 1) - self.cells // 2).astype(F32)

    def limit(self, p):
        off_z, off_x = self.off(p), float(p - self.patch) - self.first
        radius = 3 * self.patch // 2
        return float(radius * radius) - off_x * off_x - off_z * off_z

    def limits(self, plane_sets, out_ref):
        every = {p: self.limit(p) for p in sorted(set().union(*plane_sets))}
        for n, planes in enumerate(plane_sets):
            for odd in range(2):
                value = jnp.full((self.share, self.cells), -1.0, F32)
                for p in planes:
                    if p % 2 == odd:
                        value = jnp.maximum(value, every[p])
                out_ref[n, odd] = value.astype(BF)

    def gaps(self, gap_ref):
        row = self.second.astype(I32)
        for s in range(self.slots):
            ahead = s - row + self.slots // 2
            off = (jnp.bitwise_and(ahead, self.slots - 1) - self.slots // 2).astype(F32)
            gap_ref[0, s] = (off * off).astype(BF)
            gap_ref[1, s] = (jnp.bitwise_and(ahead, self.total_rows - 1) < self.slots).astype(F32).astype(BF)

    def packed(self, s, part):
        value = self.ref[s, part, :]
        turn = STEP * self.patch * self.hop
        even = pltpu.roll(value, turn % self.cells, 1) if turn % self.cells else value
        return even, pltpu.roll(value, (turn + self.cells // 2) % self.cells, 1)

    def parts(self, size):
        return [slice(c, c + size) for c in range(0, self.share, size)]


def tighten(source, gap_ref, planes, o_ref):
    half = source.slots // 2
    cells = source.cells
    limits = {p: source.limit(p).astype(BF) for p in planes}
    turn = (PAIR_SKEW - SKEW) % cells
    rows = []
    for r in range(half):
        total = None
        for later in range(2):
            s = r + half * later
            value, gap = source.ref[s], gap_ref[0, s]
            some = None
            for p in reversed(planes):
                piece = jnp.where(gap <= limits[p], value, jnp.zeros_like(value))
                some = piece if some is None else piece + pltpu.roll(some, turn, 1)
            total = total + pltpu.roll(some, PAIR_ROW, 1) if later else some
        rows.append(total + pltpu.roll(total, cells // 2, 1))
    lane = iota((source.share, cells), 1)
    for u in range(half // 2):
        o_ref[u] = jnp.where(lane < cells // 2, rows[u], rows[u + half // 2])
    o_ref[half // 2] = source.ref[source.ref.shape[0] - 1]


def loosen_kernel(low_ref, up_ref, low_out_ref, up_out_ref, gap_ref, *, patch, total_rows):
    for ref, o_ref, planes in ((low_ref, low_out_ref, range(2 * patch, 3 * patch - 1)), (up_ref, up_out_ref, range(1, patch))):
        source = Source(ref, 0, patch, total_rows, SKEW)
        source.gaps(gap_ref)
        cells, half = source.cells, source.slots // 2
        limits = {p: source.limit(p).astype(BF) for p in planes}
        lane = iota((source.share, cells), 1)
        for u in range(half // 2):
            value = ref[u]
            turned = pltpu.roll(value, cells // 2, 1)
            for group in range(2):
                both = jnp.where(lane < cells // 2, *((value, turned) if group == 0 else (turned, value)))
                for later in range(2):
                    s = u + half // 2 * group + half * later
                    gap = gap_ref[0, s]
                    total = jnp.zeros_like(value)
                    for p in planes:
                        turn = (SKEW - PAIR_SKEW) * (p - planes[0]) - PAIR_ROW * later
                        total = jnp.where(gap <= limits[p], pltpu.roll(both, turn % cells, 1) if turn else both, total)
                    o_ref[s] = total
        o_ref[source.slots] = ref[half // 2]


def loosen(low, up, patch, total_rows):
    slots = total_rows // 2
    vm = pl.BlockSpec(memory_space=pltpu.VMEM)
    return pl.pallas_call(
        functools.partial(loosen_kernel, patch=patch, total_rows=total_rows),
        in_specs=[vm] * 2,
        out_specs=[vm] * 2,
        out_shape=[jax.ShapeDtypeStruct((slots + 1, *low.shape[1:]), BF)] * 2,
        scratch_shapes=[pltpu.VMEM((2, slots, *low.shape[1:]), BF)],
        compiler_params=pltpu.CompilerParams(vmem_limit_bytes=16 * 2**20),
        cost_estimate=pl.CostEstimate(flops=10**6, bytes_accessed=10**4, transcendentals=0),
    )(low, up)


def inside(gap, limit_ref, n, part, even, odd):
    zero = jnp.zeros_like(even)
    return jnp.where(gap <= limit_ref[n, 0, part, :], even, jnp.where(gap <= limit_ref[n, 1, part, :], odd, zero))


def planes_of(quads, allowed, patch, shift):
    return [[p for p in range(patch * q + shift, patch * (q + 1) + shift) if p in allowed] for q in quads]


def spread_rows(source, limit_ref, gap_ref, quads, store):
    def body(n, carry):
        for part in source.parts(A_PART):
            found = []
            for step in range(A_STEP):
                s = n * A_STEP + step
                even, odd = source.packed(s, part)
                gap = gap_ref[0, s, part, :]
                is_low = gap_ref[1, s, part, :] > 0.5
                zero = jnp.zeros_like(even)
                for n_q, q in enumerate(quads):
                    value = inside(gap, limit_ref, n_q, part, even, odd)
                    found.append((q, s, part, jnp.where(is_low, value, zero)))
                    found.append((q, s + source.slots, part, jnp.where(is_low, zero, value)))
            for item in found:
                store(*item)
        return carry

    lax.fori_loop(0, source.slots // A_STEP, body, 0, unroll=A_UNROLL)


def columns(source, allowed, limit_ref, gap_ref, group_ref, v_ref, store):
    patch, cells, share, slots = source.patch, source.cells, source.share, source.slots
    shift = -patch * source.hop
    quads = sorted({(p - shift) // patch for p in allowed})
    sets = planes_of(quads, allowed, patch, shift) + planes_of(quads, allowed, patch, shift - 1) + planes_of(quads, allowed, patch, shift + 1)
    source.limits(sets, limit_ref)
    source.gaps(gap_ref)
    count = len(quads)
    for n, q in enumerate(quads):
        group = jnp.zeros((share, cells), F32)
        for g in range(1, patch):
            group = jnp.where(jnp.abs(source.off(patch * q + shift + g)) <= float(NEAR), float(g), group)
        group_ref[n] = group

    for part in source.parts(S_PART):

        def look(s, part=part):
            even, odd = source.packed(s, part)
            gap = gap_ref[0, s, part, :]
            return even, odd, [inside(gap, limit_ref, n, part, even, odd) for n in range(count)]

        def wide(values):
            return [value.astype(F32) for value in values]

        def body(s, carry, part=part):
            before, even, odd, now = carry
            next_even, next_odd, after = look(jnp.bitwise_and(s + 1, slots - 1))
            gap = gap_ref[0, s, part, :]
            low = gap_ref[1, s, part, :]
            low_packed = low > 0.5
            low_wide = low.astype(F32) > 0.5
            found = []
            for n, q in enumerate(quads):
                value = now[n]
                below = pltpu.roll(inside(gap, limit_ref, count + n, part, even, odd), STEP, 1)
                above = pltpu.roll(inside(gap, limit_ref, 2 * count + n, part, even, odd), cells - STEP, 1)
                beside = below.astype(F32) + above.astype(F32)
                beside = beside + (before[n].astype(F32) + after[n].astype(F32))
                beside = beside + (pltpu.roll(value, 1, 1).astype(F32) + pltpu.roll(value, cells - 1, 1).astype(F32))
                group = group_ref[n, part, :]
                field = None
                for g in range(patch):
                    row = jnp.where(low_wide, *(v_ref[patch * q + g, pl.ds(y, 1), :] for y in (s, s + slots)))
                    field = row if g == 0 else jnp.where(group == float(g), row, field)
                centre = value.astype(F32)
                applied = (0.5 * (6.0 * centre - beside) + field * centre).astype(BF)
                zero = jnp.zeros_like(value)
                found.append((q, 0, s, part, jnp.where(low_packed, value, zero)))
                found.append((q, 0, s + slots, part, jnp.where(low_packed, zero, value)))
                found.append((q, 1, s, part, jnp.where(low_packed, applied, zero)))
                found.append((q, 1, s + slots, part, jnp.where(low_packed, zero, applied)))
            for item in found:
                store(*item)
            return now, next_even, next_odd, after

        lax.fori_loop(0, slots, body, (look(slots - 1)[2], *look(0)), unroll=S_UNROLL)


def row_of(y, cells):
    return pl.ds(pl.multiple_of(y * cells, cells), cells)


def product_of(b, a):
    return lax.dot_general(b, a, (((1,), (1,)), ((), ())), preferred_element_type=F32)


def own_kernel(ids_ref, own_ref, *rest, patch, total_rows, parts):
    field_refs, (b_ref, v_ref, limit_ref, gap_ref, group_ref) = rest[:parts], rest[parts:]
    m = ids_ref[0]
    share, cells = own_ref.shape[1:]
    rows = total_rows // parts
    for hop, ref in enumerate(field_refs):
        to = pl.ds(pl.multiple_of(jnp.bitwise_xor(m, hop) * rows, rows), rows)
        for p in range(3 * patch):
            v_ref[p, to, :] = pltpu.roll(ref[p], STEP * p % cells, 1) if p else ref[p]

    def store_column(q, applied, y, part, value):
        at = applied * share
        b_ref[q, at + part.start : at + part.stop, row_of(y, cells)] = value

    source = Source(own_ref, 0, patch, total_rows)
    every = range(1, 3 * patch - 1)
    columns(source, every, limit_ref, gap_ref, group_ref, v_ref, store_column)


def rows_kernel(ids_ref, *refs, patch, total_rows, parts):
    row_refs, (b_ref, a_ref, sum_ref, limit_ref, gap_ref) = refs[:parts], refs[parts:]
    share, cells = row_refs[0].shape[1:]
    every = range(1, 3 * patch - 1)
    for n, ref in enumerate(row_refs):
        who = jnp.bitwise_xor(jnp.bitwise_and(ids_ref[0], 2), n) * share
        source = Source(ref, 0, patch, total_rows)
        source.limits(planes_of(range(3), every, patch, 0), limit_ref)
        source.gaps(gap_ref)

        def store_row(q, y, part, value, who=who):
            size = part.stop - part.start
            a_ref[q, pl.ds(pl.multiple_of(who + part.start, size), size), row_of(y, cells)] = value

        spread_rows(source, limit_ref, gap_ref, range(3), store_row)
    total = product_of(b_ref[0], a_ref[0])
    for q in range(1, 3):
        total = total + product_of(b_ref[q], a_ref[q])
    sum_ref[...] = total


def others_kernel(
    ids_ref, pairs_ref, row_third_ref, own_ref, low2_ref, low1_ref, up1_ref, up2_ref, a_ref, v_ref, sum_ref,
    gram_ref, ham_ref,
    b_ref, limit_ref, gap_ref, group_ref,
    *, patch, total_rows,
):
    m = ids_ref[0]
    slots = total_rows // 2
    share, cells = own_ref.shape[1:]
    both = 2 * share
    window = 3 * patch
    spots = {}
    for hop, ref, allowed in (
        (-1, low1_ref, range(patch, window - 1)),
        (1, up1_ref, range(1, 2 * patch)),
        (-2, low2_ref, range(2 * patch, window - 1)),
        (2, up2_ref, range(1, patch)),
    ):
        def store_column(q, applied, y, part, value, hop=hop):
            taken = sorted({q - 2, q - 1, q} - {0}).index(hop)
            spots[hop, q] = taken
            at = taken * both + applied * share
            b_ref[q, at + part.start : at + part.stop, row_of(y, cells)] = value

        source = Source(ref, hop, patch, total_rows)
        columns(source, allowed, limit_ref, gap_ref, group_ref, v_ref, store_column)

    sums = {0: sum_ref[...]}
    for q in range(3):
        product = product_of(b_ref[q], a_ref[q])
        for (hop, at_q), taken in spots.items():
            if at_q == q:
                piece = product[taken * both : (taken + 1) * both]
                sums[hop] = piece if hop not in sums else sums[hop] + piece

    orbs = a_ref.shape[1]
    half_rows = orbs // pairs_ref.shape[0]
    column_block = (m * share) // half_rows
    row_third = row_third_ref[...]
    row_block = iota((1, orbs), 1) // half_rows
    for k, ref in enumerate((low2_ref, low1_ref, own_ref, up1_ref, up2_ref)):
        column_third = ref[slots].astype(F32)[:, 2:3]
        weight = jnp.zeros((1, orbs), F32)
        for g in range(pairs_ref.shape[0]):
            weight = jnp.where(row_block == g, pairs_ref[g, k, column_block].astype(F32), weight)
        weight = jnp.where(jnp.abs(row_third - column_third) <= float(NEAR), weight, 0.0)
        gram_ref[k] = sums[k - 2][:share] * weight
        ham_ref[k] = sums[k - 2][share:] * weight


def products(ids, pairs, row_third, own, rows, others, fields, patch, total_rows, orbs):
    share, cells = rows[0].shape[1:]
    slots = total_rows // 2
    long = total_rows * cells
    vm = pl.BlockSpec(memory_space=pltpu.VMEM)
    sm = pl.BlockSpec(memory_space=pltpu.SMEM)
    params = pltpu.CompilerParams(vmem_limit_bytes=26 * 2**20)
    cost = pl.CostEstimate(flops=10**6, bytes_accessed=10**4, transcendentals=0)
    sizes = dict(patch=patch, total_rows=total_rows)

    def scratch(quads):
        return [
            pltpu.VMEM((3 * quads, 2, share, cells), BF),
            pltpu.VMEM((2, slots, share, cells), BF),
            pltpu.VMEM((quads, share, cells), F32),
        ]

    b, v = pl.pallas_call(
        functools.partial(own_kernel, **sizes, parts=len(rows)),
        in_specs=[sm] + [vm] * (1 + len(fields)),
        out_specs=[vm] * 2,
        out_shape=[jax.ShapeDtypeStruct((3, 2 * share, long), BF), jax.ShapeDtypeStruct((3 * patch, total_rows, cells), F32)],
        scratch_shapes=scratch(3),
        compiler_params=params,
        cost_estimate=cost,
    )(ids, own, *fields)
    a, own_sum = pl.pallas_call(
        functools.partial(rows_kernel, **sizes, parts=len(rows)),
        in_specs=[sm] + [vm] * (len(rows) + 1),
        out_specs=[vm] * 2,
        out_shape=[jax.ShapeDtypeStruct((3, orbs, long), BF), jax.ShapeDtypeStruct((2 * share, orbs), F32)],
        scratch_shapes=[pltpu.VMEM((3, 2, share, cells), BF), pltpu.VMEM((2, slots, share, cells), BF)],
        compiler_params=params,
        cost_estimate=cost,
    )(ids, *rows, b)
    out = jax.ShapeDtypeStruct((5, share, orbs), F32)
    return pl.pallas_call(
        functools.partial(others_kernel, **sizes),
        in_specs=[sm, sm] + [vm] * 9,
        out_specs=[vm, vm],
        out_shape=[out, out],
        scratch_shapes=[pltpu.VMEM((3, 4 * share, long), BF)] + scratch(2),
        compiler_params=params,
        cost_estimate=cost,
    )(ids, pairs, row_third, own, *others, a, v, own_sum)


def hop(x, k):
    return lax.ppermute(x, "mat", [(i, i ^ k) for i in range(lax.axis_size("mat"))])


def along(x, distance):
    size = lax.axis_size("dom")
    return lax.ppermute(x, "dom", [((i - distance) % size, i) for i in range(size)])


def on_device(orbitals, potential, centre_first, centre_second, centre_third, correlation_pairs):
    orbs, window, rows, cells = orbitals.shape
    patch = potential.shape[0]
    parts = lax.axis_size("mat")
    ids = lax.axis_index("mat")[None]

    centres = jnp.stack([centre_first, centre_second, centre_third])
    away, home = pack(ids, centres, orbitals, parts, patch)
    before, after = along(potential, 1), along(potential, -1)
    away, home, before, after = lax.optimization_barrier((away, home, before, after))
    far_home, far_away = hop(away, 2), hop(home, 2)
    near_home, near_away = hop(home, 1), hop(away, 1)
    field = jnp.concatenate([before, potential, after], axis=0)
    far_field = hop(field, 2)
    far_home, far_field = lax.optimization_barrier((far_home, far_field))
    centres = centres.T.astype(F32)
    share = orbs // parts
    homes = (home, near_home, far_home, hop(far_home, 1))
    merged, low2, up2 = merge_rows(ids, centres, share, patch, True, homes)
    low2, low1, up1, up2 = along(low2, 2), along(merged, 1), along(merged, -1), along(up2, -2)
    far_away, low2, up2 = lax.optimization_barrier((far_away, low2, up2))
    fields = (field, hop(field, 1), far_field, hop(far_field, 1))
    every = merge_rows(ids, centres, share, patch, False, homes, (away, near_away, far_away, hop(far_away, 1)))
    low2, up2 = loosen(low2, up2, patch, rows * parts)
    others = (low2, low1, up1, up2)
    row_third = centre_third.astype(F32)[None, :]
    return tuple(products(ids, correlation_pairs, row_third, merged, every, others, fields, patch, rows * parts, orbs))


def solution(mesh):
    return jax.shard_map(
        on_device,
        mesh=mesh,
        in_specs=(
            P("dom", None, "mat", None),
            P("dom", "mat", None),
            P("dom"),
            P("dom"),
            P("dom"),
            P("dom", None, None),
        ),
        out_specs=(P(None, "mat", "dom"), P(None, "mat", "dom")),
        check_vma=False,
    )
```

```python
import functools

import jax
import jax.numpy as jnp
from jax import lax
from jax.experimental import pallas as pl
from jax.experimental.pallas import tpu as pltpu
from jax.sharding import PartitionSpec as P

STEP = 29
SKEW = STEP + 64
NEAR = 14
PAIR_SKEW, PAIR_ROW = 22, 32
P_STEP, P_UNROLL = 16, 1
A_PART, A_STEP, A_UNROLL = 16, 8, 1
S_PART, S_UNROLL = 32, 16
BF = jnp.bfloat16
F32 = jnp.float32
I32 = jnp.int32


def iota(shape, axis):
    return lax.broadcasted_iota(I32, shape, axis)


def half_of(m, own):
    return jnp.bitwise_xor(m // 2, 1 - own)


def pack_kernel(ids_ref, centre_in, x_ref, o_ref, landed, arrived, limits, scr, centre_ref, told, *, own, patch, rows, total_rows):
    _, half, cells = o_ref.shape
    steps, count = landed.shape[:2]
    window = 3 * patch
    pairs = window // 2
    radius = window // 2
    m = ids_ref[0]

    def start_of(step):
        return pl.multiple_of(half_of(m, own) * half + step * count, count)

    copies = []
    for step in range(steps):
        copies.append(pltpu.make_async_copy(x_ref.at[pl.ds(start_of(step), count)], landed.at[step], arrived.at[step]))
        copies[-1].start()
    centre_copy = pltpu.make_async_copy(centre_in, centre_ref, told.at[0])
    centre_copy.start()

    plane = iota((2 * rows, cells), 0) // rows
    for a in range(pairs):
        p = plane + 2 * a
        inside = (p >= 1) & (p <= window - 2)
        for first in range(patch):
            off = p - patch - first
            limits[first, a] = jnp.where(inside, radius * radius - off * off, -1).astype(F32).astype(BF)
    z = iota((rows, cells), 1).astype(F32)
    y = (iota((rows, cells), 0) + m * rows).astype(F32)

    centre_copy.wait()
    for step in range(steps):
        copies[step].wait()

        def body(n, carry, base=start_of(step), step=step):
            found = []
            for i in range(P_STEP):
                at = n * P_STEP + i
                first = centre_ref[0, base + at]
                off_z = z - centre_ref[2, base + at].astype(F32)
                off_y = jnp.abs(y - centre_ref[1, base + at].astype(F32))
                off_y = jnp.minimum(off_y, float(total_rows) - off_y)
                distance = off_z * off_z + off_y * off_y
                distance = jnp.concatenate([distance, distance], axis=0).astype(BF)
                total = None
                for a in range(pairs):
                    x = landed[step, at, 2 * a * rows : 2 * (a + 1) * rows, :]
                    x = jnp.where(distance <= limits[first, a], x, jnp.zeros_like(x))
                    turn = 2 * SKEW * a % cells
                    total = x if total is None else total + pltpu.roll(x, turn, 1)
                odd = pltpu.roll(total, SKEW, 1)
                found.append((at, total.astype(F32)[:rows] + odd.astype(F32)[rows:]))
            for at, value in found:
                scr[at] = value
            return carry

        lax.fori_loop(0, count // P_STEP, body, 0, unroll=P_UNROLL)
        for r in range(rows):
            o_ref[r, step * count : (step + 1) * count, :] = scr[:, r, :].astype(BF)


def pack(ids, centres, orbitals, parts, patch, own):
    orbs, window, rows, cells = orbitals.shape
    half, steps = orbs // 2, 4
    count = half // steps
    sm = pl.BlockSpec(memory_space=pltpu.SMEM)
    return pl.pallas_call(
        functools.partial(pack_kernel, own=own, patch=patch, rows=rows, total_rows=rows * parts),
        in_specs=[sm] + [pl.BlockSpec(memory_space=pl.ANY)] * 2,
        out_specs=pl.BlockSpec(memory_space=pltpu.VMEM),
        out_shape=jax.ShapeDtypeStruct((rows, half, cells), BF),
        scratch_shapes=[
            pltpu.VMEM((steps, count, window * rows, cells), BF),
            pltpu.SemaphoreType.DMA((steps,)),
            pltpu.VMEM((patch, window // 2, 2 * rows, cells), BF),
            pltpu.VMEM((count, rows, cells), F32),
            pltpu.SMEM(centres.shape, I32),
            pltpu.SemaphoreType.DMA((1,)),
        ],
        compiler_params=pltpu.CompilerParams(vmem_limit_bytes=53 * 2**20),
        cost_estimate=pl.CostEstimate(flops=orbitals.size * 256, bytes_accessed=orbitals.size, transcendentals=0),
    )(ids, centres, orbitals.reshape(orbs, window * rows, cells))


def merge_kernel(ids_ref, centre_ref, *refs, chips, own_only, patch):
    m = ids_ref[0]
    parity = m % 2
    o_refs = refs[4 * chips :]
    share = o_refs[0].shape[1]
    for chip in range(chips):
        own_ref, near_ref, far_ref, diag_ref = refs[4 * chip : 4 * chip + 4]
        rows, half, cells = own_ref.shape
        for n in [None] if own_only else range(half // share):
            o_ref = o_refs[0] if own_only else o_refs[chip * half // share + n]
            start = parity * share if own_only else n * share
            source = pl.ds(pl.multiple_of(start, share), share)
            centres = centre_ref[pl.ds(pl.multiple_of(half_of(m, 1 - chip) * half + start, share), share), :]
            lane = iota((share, cells), 1)
            meta = jnp.where(lane == 0, centres[:, 0:1], jnp.where(lane == 1, centres[:, 1:2], centres[:, 2:3]))
            o_ref[pl.ds(parity * rows, rows)] = own_ref[:, source, :] + far_ref[:, source, :]
            o_ref[pl.ds((1 - parity) * rows, rows)] = near_ref[:, source, :] + diag_ref[:, source, :]
            o_ref[2 * rows] = meta.astype(BF)
    if own_only:
        o_ref, low_ref, up_ref, gap_ref = o_refs
        source = Source(o_ref, 0, patch, 4 * rows, SKEW)
        source.gaps(gap_ref)
        tighten(source, gap_ref, range(2 * patch, 3 * patch - 1), low_ref)
        tighten(source, gap_ref, range(1, patch), up_ref)


def merge_rows(ids, centres, share, patch, own_only, *packs):
    rows, half, cells = packs[0][0].shape
    units = [2 * rows + 1, rows // 2 + 1, rows // 2 + 1] if own_only else [2 * rows + 1] * (len(packs) * half // share)
    return pl.pallas_call(
        functools.partial(merge_kernel, chips=len(packs), own_only=own_only, patch=patch),
        in_specs=[pl.BlockSpec(memory_space=pltpu.SMEM)] + [pl.BlockSpec(memory_space=pltpu.VMEM)] * (1 + 4 * len(packs)),
        out_specs=[pl.BlockSpec(memory_space=pltpu.VMEM)] * len(units),
        out_shape=[jax.ShapeDtypeStruct((n, share, cells), BF) for n in units],
        scratch_shapes=[pltpu.VMEM((2, 2 * rows, share, cells), BF)] if own_only else [],
        compiler_params=pltpu.CompilerParams(vmem_limit_bytes=16 * 2**20),
    )(ids, centres, *(array for pack in packs for array in pack))


class Source:
    def __init__(self, ref, hop, patch, total_rows, step=STEP):
        self.ref, self.hop, self.patch, self.total_rows, self.step = ref, hop, patch, total_rows, step
        self.slots = total_rows // 2
        units, self.share, self.cells = ref.shape
        meta = ref[units - 1].astype(F32)
        shape = (self.share, self.cells)
        self.first, self.second, self.third = (jnp.broadcast_to(meta[:, c : c + 1], shape) for c in range(3))
        self.start = iota(shape, 1) - self.third.astype(I32) + self.cells // 2

    def off(self, p):
        place = self.step * (p + self.patch * self.hop)
        return (jnp.bitwise_and(self.start - place, self.cells - 1) - self.cells // 2).astype(F32)

    def limit(self, p):
        off_z, off_x = self.off(p), float(p - self.patch) - self.first
        radius = 3 * self.patch // 2
        return float(radius * radius) - off_x * off_x - off_z * off_z

    def limits(self, plane_sets, out_ref):
        every = {p: self.limit(p) for p in sorted(set().union(*plane_sets))}
        for n, planes in enumerate(plane_sets):
            for odd in range(2):
                value = jnp.full((self.share, self.cells), -1.0, F32)
                for p in planes:
                    if p % 2 == odd:
                        value = jnp.maximum(value, every[p])
                out_ref[n, odd] = value.astype(BF)

    def gaps(self, gap_ref):
        row = self.second.astype(I32)
        for s in range(self.slots):
            ahead = s - row + self.slots // 2
            off = (jnp.bitwise_and(ahead, self.slots - 1) - self.slots // 2).astype(F32)
            gap_ref[0, s] = (off * off).astype(BF)
            gap_ref[1, s] = (jnp.bitwise_and(ahead, self.total_rows - 1) < self.slots).astype(F32).astype(BF)

    def packed(self, s, part):
        value = self.ref[s, part, :]
        turn = STEP * self.patch * self.hop
        even = pltpu.roll(value, turn % self.cells, 1) if turn % self.cells else value
        return even, pltpu.roll(value, (turn + self.cells // 2) % self.cells, 1)

    def parts(self, size):
        return [slice(c, c + size) for c in range(0, self.share, size)]


def tighten(source, gap_ref, planes, o_ref):
    half = source.slots // 2
    cells = source.cells
    limits = {p: source.limit(p).astype(BF) for p in planes}
    turn = (PAIR_SKEW - SKEW) % cells
    rows = []
    for r in range(half):
        total = None
        for later in range(2):
            s = r + half * later
            value, gap = source.ref[s], gap_ref[0, s]
            some = None
            for p in reversed(planes):
                piece = jnp.where(gap <= limits[p], value, jnp.zeros_like(value))
                some = piece if some is None else piece + pltpu.roll(some, turn, 1)
            total = total + pltpu.roll(some, PAIR_ROW, 1) if later else some
        rows.append(total + pltpu.roll(total, cells // 2, 1))
    lane = iota((source.share, cells), 1)
    for u in range(half // 2):
        o_ref[u] = jnp.where(lane < cells // 2, rows[u], rows[u + half // 2])
    o_ref[half // 2] = source.ref[source.ref.shape[0] - 1]


def loosen_kernel(low_ref, up_ref, low_out_ref, up_out_ref, gap_ref, *, patch, total_rows):
    for ref, o_ref, planes in ((low_ref, low_out_ref, range(2 * patch, 3 * patch - 1)), (up_ref, up_out_ref, range(1, patch))):
        source = Source(ref, 0, patch, total_rows, SKEW)
        source.gaps(gap_ref)
        cells, half = source.cells, source.slots // 2
        limits = {p: source.limit(p).astype(BF) for p in planes}
        lane = iota((source.share, cells), 1)
        for u in range(half // 2):
            value = ref[u]
            turned = pltpu.roll(value, cells // 2, 1)
            for group in range(2):
                both = jnp.where(lane < cells // 2, *((value, turned) if group == 0 else (turned, value)))
                for later in range(2):
                    s = u + half // 2 * group + half * later
                    gap = gap_ref[0, s]
                    total = jnp.zeros_like(value)
                    for p in planes:
                        turn = (SKEW - PAIR_SKEW) * (p - planes[0]) - PAIR_ROW * later
                        total = jnp.where(gap <= limits[p], pltpu.roll(both, turn % cells, 1) if turn else both, total)
                    o_ref[s] = total
        o_ref[source.slots] = ref[half // 2]


def loosen(low, up, patch, total_rows):
    slots = total_rows // 2
    vm = pl.BlockSpec(memory_space=pltpu.VMEM)
    return pl.pallas_call(
        functools.partial(loosen_kernel, patch=patch, total_rows=total_rows),
        in_specs=[vm] * 2,
        out_specs=[vm] * 2,
        out_shape=[jax.ShapeDtypeStruct((slots + 1, *low.shape[1:]), BF)] * 2,
        scratch_shapes=[pltpu.VMEM((2, slots, *low.shape[1:]), BF)],
        compiler_params=pltpu.CompilerParams(vmem_limit_bytes=16 * 2**20),
        cost_estimate=pl.CostEstimate(flops=10**6, bytes_accessed=10**4, transcendentals=0),
    )(low, up)


def inside(gap, limit_ref, n, part, even, odd):
    zero = jnp.zeros_like(even)
    return jnp.where(gap <= limit_ref[n, 0, part, :], even, jnp.where(gap <= limit_ref[n, 1, part, :], odd, zero))


def planes_of(quads, allowed, patch, shift):
    return [[p for p in range(patch * q + shift, patch * (q + 1) + shift) if p in allowed] for q in quads]


def spread_rows(source, limit_ref, gap_ref, quads, store):
    def body(n, carry):
        for part in source.parts(A_PART):
            found = []
            for step in range(A_STEP):
                s = n * A_STEP + step
                even, odd = source.packed(s, part)
                gap = gap_ref[0, s, part, :]
                is_low = gap_ref[1, s, part, :] > 0.5
                zero = jnp.zeros_like(even)
                for n_q, q in enumerate(quads):
                    value = inside(gap, limit_ref, n_q, part, even, odd)
                    found.append((q, s, part, jnp.where(is_low, value, zero)))
                    found.append((q, s + source.slots, part, jnp.where(is_low, zero, value)))
            for item in found:
                store(*item)
        return carry

    lax.fori_loop(0, source.slots // A_STEP, body, 0, unroll=A_UNROLL)


def columns(source, allowed, limit_ref, gap_ref, group_ref, v_ref, store):
    patch, cells, share, slots = source.patch, source.cells, source.share, source.slots
    shift = -patch * source.hop
    quads = sorted({(p - shift) // patch for p in allowed})
    sets = planes_of(quads, allowed, patch, shift) + planes_of(quads, allowed, patch, shift - 1) + planes_of(quads, allowed, patch, shift + 1)
    source.limits(sets, limit_ref)
    source.gaps(gap_ref)
    count = len(quads)
    for n, q in enumerate(quads):
        group = jnp.zeros((share, cells), F32)
        for g in range(1, patch):
            group = jnp.where(jnp.abs(source.off(patch * q + shift + g)) <= float(NEAR), float(g), group)
        group_ref[n] = group

    for part in source.parts(S_PART):

        def look(s, part=part):
            even, odd = source.packed(s, part)
            gap = gap_ref[0, s, part, :]
            return even, odd, [inside(gap, limit_ref, n, part, even, odd) for n in range(count)]

        def wide(values):
            return [value.astype(F32) for value in values]

        def body(s, carry, part=part):
            before, even, odd, now = carry
            next_even, next_odd, after = look(jnp.bitwise_and(s + 1, slots - 1))
            gap = gap_ref[0, s, part, :]
            low = gap_ref[1, s, part, :]
            low_packed = low > 0.5
            low_wide = low.astype(F32) > 0.5
            found = []
            for n, q in enumerate(quads):
                value = now[n]
                below = pltpu.roll(inside(gap, limit_ref, count + n, part, even, odd), STEP, 1)
                above = pltpu.roll(inside(gap, limit_ref, 2 * count + n, part, even, odd), cells - STEP, 1)
                beside = below.astype(F32) + above.astype(F32)
                beside = beside + (before[n].astype(F32) + after[n].astype(F32))
                beside = beside + (pltpu.roll(value, 1, 1).astype(F32) + pltpu.roll(value, cells - 1, 1).astype(F32))
                group = group_ref[n, part, :]
                field = None
                for g in range(patch):
                    row = jnp.where(low_wide, *(v_ref[patch * q + g, pl.ds(y, 1), :] for y in (s, s + slots)))
                    field = row if g == 0 else jnp.where(group == float(g), row, field)
                centre = value.astype(F32)
                applied = (0.5 * (6.0 * centre - beside) + field * centre).astype(BF)
                zero = jnp.zeros_like(value)
                found.append((q, 0, s, part, jnp.where(low_packed, value, zero)))
                found.append((q, 0, s + slots, part, jnp.where(low_packed, zero, value)))
                found.append((q, 1, s, part, jnp.where(low_packed, applied, zero)))
                found.append((q, 1, s + slots, part, jnp.where(low_packed, zero, applied)))
            for item in found:
                store(*item)
            return now, next_even, next_odd, after

        lax.fori_loop(0, slots, body, (look(slots - 1)[2], *look(0)), unroll=S_UNROLL)


def row_of(y, cells):
    return pl.ds(pl.multiple_of(y * cells, cells), cells)


def product_of(b, a):
    return lax.dot_general(b, a, (((1,), (1,)), ((), ())), preferred_element_type=F32)


def own_kernel(ids_ref, own_ref, *rest, patch, total_rows, parts):
    field_refs, (b_ref, v_ref, limit_ref, gap_ref, group_ref) = rest[:parts], rest[parts:]
    m = ids_ref[0]
    share, cells = own_ref.shape[1:]
    rows = total_rows // parts
    for hop, ref in enumerate(field_refs):
        to = pl.ds(pl.multiple_of(jnp.bitwise_xor(m, hop) * rows, rows), rows)
        for p in range(3 * patch):
            v_ref[p, to, :] = pltpu.roll(ref[p], STEP * p % cells, 1) if p else ref[p]

    def store_column(q, applied, y, part, value):
        at = applied * share
        b_ref[q, at + part.start : at + part.stop, row_of(y, cells)] = value

    source = Source(own_ref, 0, patch, total_rows)
    every = range(1, 3 * patch - 1)
    columns(source, every, limit_ref, gap_ref, group_ref, v_ref, store_column)


def rows_kernel(ids_ref, *refs, patch, total_rows, parts):
    row_refs, (b_ref, a_ref, sum_ref, limit_ref, gap_ref) = refs[:parts], refs[parts:]
    share, cells = row_refs[0].shape[1:]
    every = range(1, 3 * patch - 1)
    for n, ref in enumerate(row_refs):
        who = jnp.bitwise_xor(jnp.bitwise_and(ids_ref[0], 2), n) * share
        source = Source(ref, 0, patch, total_rows)
        source.limits(planes_of(range(3), every, patch, 0), limit_ref)
        source.gaps(gap_ref)

        def store_row(q, y, part, value, who=who):
            size = part.stop - part.start
            a_ref[q, pl.ds(pl.multiple_of(who + part.start, size), size), row_of(y, cells)] = value

        spread_rows(source, limit_ref, gap_ref, range(3), store_row)
    total = product_of(b_ref[0], a_ref[0])
    for q in range(1, 3):
        total = total + product_of(b_ref[q], a_ref[q])
    sum_ref[...] = total


def others_kernel(
    ids_ref, pairs_ref, row_third_ref, own_ref, low2_ref, low1_ref, up1_ref, up2_ref, a_ref, v_ref, sum_ref,
    gram_ref, ham_ref,
    b_ref, limit_ref, gap_ref, group_ref,
    *, patch, total_rows,
):
    m = ids_ref[0]
    slots = total_rows // 2
    share, cells = own_ref.shape[1:]
    both = 2 * share
    window = 3 * patch
    spots = {}
    for hop, ref, allowed in (
        (-1, low1_ref, range(patch, window - 1)),
        (1, up1_ref, range(1, 2 * patch)),
        (-2, low2_ref, range(2 * patch, window - 1)),
        (2, up2_ref, range(1, patch)),
    ):
        def store_column(q, applied, y, part, value, hop=hop):
            taken = sorted({q - 2, q - 1, q} - {0}).index(hop)
            spots[hop, q] = taken
            at = taken * both + applied * share
            b_ref[q, at + part.start : at + part.stop, row_of(y, cells)] = value

        source = Source(ref, hop, patch, total_rows)
        columns(source, allowed, limit_ref, gap_ref, group_ref, v_ref, store_column)

    sums = {0: sum_ref[...]}
    for q in range(3):
        product = product_of(b_ref[q], a_ref[q])
        for (hop, at_q), taken in spots.items():
            if at_q == q:
                piece = product[taken * both : (taken + 1) * both]
                sums[hop] = piece if hop not in sums else sums[hop] + piece

    orbs = a_ref.shape[1]
    half_rows = orbs // pairs_ref.shape[0]
    column_block = (m * share) // half_rows
    row_third = row_third_ref[...]
    row_block = iota((1, orbs), 1) // half_rows
    for k, ref in enumerate((low2_ref, low1_ref, own_ref, up1_ref, up2_ref)):
        column_third = ref[slots].astype(F32)[:, 2:3]
        weight = jnp.zeros((1, orbs), F32)
        for g in range(pairs_ref.shape[0]):
            weight = jnp.where(row_block == g, pairs_ref[g, k, column_block].astype(F32), weight)
        weight = jnp.where(jnp.abs(row_third - column_third) <= float(NEAR), weight, 0.0)
        gram_ref[k] = sums[k - 2][:share] * weight
        ham_ref[k] = sums[k - 2][share:] * weight


def products(ids, pairs, row_third, own, rows, others, fields, patch, total_rows, orbs):
    share, cells = rows[0].shape[1:]
    slots = total_rows // 2
    long = total_rows * cells
    vm = pl.BlockSpec(memory_space=pltpu.VMEM)
    sm = pl.BlockSpec(memory_space=pltpu.SMEM)
    params = pltpu.CompilerParams(vmem_limit_bytes=26 * 2**20)
    cost = pl.CostEstimate(flops=10**6, bytes_accessed=10**4, transcendentals=0)
    sizes = dict(patch=patch, total_rows=total_rows)

    def scratch(quads):
        return [
            pltpu.VMEM((3 * quads, 2, share, cells), BF),
            pltpu.VMEM((2, slots, share, cells), BF),
            pltpu.VMEM((quads, share, cells), F32),
        ]

    b, v = pl.pallas_call(
        functools.partial(own_kernel, **sizes, parts=len(rows)),
        in_specs=[sm] + [vm] * (1 + len(fields)),
        out_specs=[vm] * 2,
        out_shape=[jax.ShapeDtypeStruct((3, 2 * share, long), BF), jax.ShapeDtypeStruct((3 * patch, total_rows, cells), F32)],
        scratch_shapes=scratch(3),
        compiler_params=params,
        cost_estimate=cost,
    )(ids, own, *fields)
    a, own_sum = pl.pallas_call(
        functools.partial(rows_kernel, **sizes, parts=len(rows)),
        in_specs=[sm] + [vm] * (len(rows) + 1),
        out_specs=[vm] * 2,
        out_shape=[jax.ShapeDtypeStruct((3, orbs, long), BF), jax.ShapeDtypeStruct((2 * share, orbs), F32)],
        scratch_shapes=[pltpu.VMEM((3, 2, share, cells), BF), pltpu.VMEM((2, slots, share, cells), BF)],
        compiler_params=params,
        cost_estimate=cost,
    )(ids, *rows, b)
    out = jax.ShapeDtypeStruct((5, share, orbs), F32)
    return pl.pallas_call(
        functools.partial(others_kernel, **sizes),
        in_specs=[sm, sm] + [vm] * 9,
        out_specs=[vm, vm],
        out_shape=[out, out],
        scratch_shapes=[pltpu.VMEM((3, 4 * share, long), BF)] + scratch(2),
        compiler_params=params,
        cost_estimate=cost,
    )(ids, pairs, row_third, own, *others, a, v, own_sum)


def hop(x, k):
    return lax.ppermute(x, "mat", [(i, i ^ k) for i in range(lax.axis_size("mat"))])


def along(x, distance):
    size = lax.axis_size("dom")
    return lax.ppermute(x, "dom", [((i - distance) % size, i) for i in range(size)])


def on_device(orbitals, potential, centre_first, centre_second, centre_third, correlation_pairs):
    orbs, window, rows, cells = orbitals.shape
    patch = potential.shape[0]
    parts = lax.axis_size("mat")
    ids = lax.axis_index("mat")[None]

    centres = jnp.stack([centre_first, centre_second, centre_third])
    away = pack(ids, centres, orbitals, parts, patch, 0)
    before, after = along(potential, 1), along(potential, -1)
    away, before, after = lax.optimization_barrier((away, before, after))
    far_home = hop(away, 2)
    home = pack(ids, centres, orbitals, parts, patch, 1)
    far_away = hop(home, 2)
    near_home, near_away = hop(home, 1), hop(away, 1)
    field = jnp.concatenate([before, potential, after], axis=0)
    far_field, near_field = hop(field, 2), hop(field, 1)
    far_home, far_field, near_field, home = lax.optimization_barrier((far_home, far_field, near_field, home))
    diag_home, diag_field = hop(far_home, 1), hop(far_field, 1)
    diag_home, diag_field = lax.optimization_barrier((diag_home, diag_field))
    fields = (field, near_field, far_field, diag_field)
    centres = centres.T.astype(F32)
    share = orbs // parts
    homes = (home, near_home, far_home, diag_home)
    merged, low2, up2 = merge_rows(ids, centres, share, patch, True, homes)
    low2, low1, up1, up2 = along(low2, 2), along(merged, 1), along(merged, -1), along(up2, -2)
    far_away, low2, up2 = lax.optimization_barrier((far_away, low2, up2))
    every = merge_rows(ids, centres, share, patch, False, homes, (away, near_away, far_away, hop(far_away, 1)))
    low2, up2 = loosen(low2, up2, patch, rows * parts)
    others = (low2, low1, up1, up2)
    row_third = centre_third.astype(F32)[None, :]
    return tuple(products(ids, correlation_pairs, row_third, merged, every, others, fields, patch, rows * parts, orbs))


def solution(mesh):
    return jax.shard_map(
        on_device,
        mesh=mesh,
        in_specs=(
            P("dom", None, "mat", None),
            P("dom", "mat", None),
            P("dom"),
            P("dom"),
            P("dom"),
            P("dom", None, None),
        ),
        out_specs=(P(None, "mat", "dom"), P(None, "mat", "dom")),
        check_vma=False,
    )
```

```python
import functools

import jax
import jax.numpy as jnp
from jax import lax
from jax.experimental import pallas as pl
from jax.experimental.pallas import tpu as pltpu
from jax.sharding import PartitionSpec as P

STEP = 29
SKEW = STEP + 64
NEAR = 14
PAIR_SKEW, PAIR_ROW = 22, 32
P_STEP, P_UNROLL = 16, 1
A_PART, A_STEP, A_UNROLL = 16, 8, 1
S_PART, S_UNROLL = 32, 16
BF = jnp.bfloat16
F32 = jnp.float32
I32 = jnp.int32


def iota(shape, axis):
    return lax.broadcasted_iota(I32, shape, axis)


def half_of(m, own):
    return jnp.bitwise_xor(m // 2, 1 - own)


def pack_kernel(ids_ref, centre_in, x_ref, o_ref, landed, arrived, limits, scr, centre_ref, told, *, own, patch, rows, total_rows):
    _, half, cells = o_ref.shape
    steps, count = landed.shape[:2]
    window = 3 * patch
    pairs = window // 2
    radius = window // 2
    m = ids_ref[0]

    def start_of(step):
        return pl.multiple_of(half_of(m, own) * half + step * count, count)

    copies = []
    for step in range(steps):
        copies.append(pltpu.make_async_copy(x_ref.at[pl.ds(start_of(step), count)], landed.at[step], arrived.at[step]))
        copies[-1].start()
    centre_copy = pltpu.make_async_copy(centre_in, centre_ref, told.at[0])
    centre_copy.start()

    plane = iota((2 * rows, cells), 0) // rows
    for a in range(pairs):
        p = plane + 2 * a
        inside = (p >= 1) & (p <= window - 2)
        for first in range(patch):
            off = p - patch - first
            limits[first, a] = jnp.where(inside, radius * radius - off * off, -1).astype(F32).astype(BF)
    z = iota((rows, cells), 1).astype(F32)
    y = (iota((rows, cells), 0) + m * rows).astype(F32)

    centre_copy.wait()
    for step in range(steps):
        copies[step].wait()

        def body(n, carry, base=start_of(step), step=step):
            found = []
            for i in range(P_STEP):
                at = n * P_STEP + i
                first = centre_ref[0, base + at]
                off_z = z - centre_ref[2, base + at].astype(F32)
                off_y = jnp.abs(y - centre_ref[1, base + at].astype(F32))
                off_y = jnp.minimum(off_y, float(total_rows) - off_y)
                distance = off_z * off_z + off_y * off_y
                distance = jnp.concatenate([distance, distance], axis=0).astype(BF)
                total = None
                for a in range(pairs):
                    x = landed[step, at, 2 * a * rows : 2 * (a + 1) * rows, :]
                    x = jnp.where(distance <= limits[first, a], x, jnp.zeros_like(x))
                    turn = 2 * SKEW * a % cells
                    total = x if total is None else total + pltpu.roll(x, turn, 1)
                odd = pltpu.roll(total, SKEW, 1)
                found.append((at, total.astype(F32)[:rows] + odd.astype(F32)[rows:]))
            for at, value in found:
                scr[at] = value
            return carry

        lax.fori_loop(0, count // P_STEP, body, 0, unroll=P_UNROLL)
        for r in range(rows):
            o_ref[r, step * count : (step + 1) * count, :] = scr[:, r, :].astype(BF)


def pack(ids, centres, orbitals, parts, patch, own):
    orbs, window, rows, cells = orbitals.shape
    half, steps = orbs // 2, 4
    count = half // steps
    sm = pl.BlockSpec(memory_space=pltpu.SMEM)
    return pl.pallas_call(
        functools.partial(pack_kernel, own=own, patch=patch, rows=rows, total_rows=rows * parts),
        in_specs=[sm] + [pl.BlockSpec(memory_space=pl.ANY)] * 2,
        out_specs=pl.BlockSpec(memory_space=pltpu.VMEM),
        out_shape=jax.ShapeDtypeStruct((rows, half, cells), BF),
        scratch_shapes=[
            pltpu.VMEM((steps, count, window * rows, cells), BF),
            pltpu.SemaphoreType.DMA((steps,)),
            pltpu.VMEM((patch, window // 2, 2 * rows, cells), BF),
            pltpu.VMEM((count, rows, cells), F32),
            pltpu.SMEM(centres.shape, I32),
            pltpu.SemaphoreType.DMA((1,)),
        ],
        compiler_params=pltpu.CompilerParams(vmem_limit_bytes=53 * 2**20),
        cost_estimate=pl.CostEstimate(flops=orbitals.size * 256, bytes_accessed=orbitals.size, transcendentals=0),
    )(ids, centres, orbitals.reshape(orbs, window * rows, cells))


def merge_kernel(ids_ref, centre_ref, *refs, chips, own_only, patch):
    m = ids_ref[0]
    parity = m % 2
    o_refs = refs[4 * chips :]
    share = o_refs[0].shape[1]
    for chip in range(chips):
        own_ref, near_ref, far_ref, diag_ref = refs[4 * chip : 4 * chip + 4]
        rows, half, cells = own_ref.shape
        for n in [None] if own_only else range(half // share):
            o_ref = o_refs[0] if own_only else o_refs[chip * half // share + n]
            start = parity * share if own_only else n * share
            source = pl.ds(pl.multiple_of(start, share), share)
            centres = centre_ref[pl.ds(pl.multiple_of(half_of(m, 1 - chip) * half + start, share), share), :]
            lane = iota((share, cells), 1)
            meta = jnp.where(lane == 0, centres[:, 0:1], jnp.where(lane == 1, centres[:, 1:2], centres[:, 2:3]))
            o_ref[pl.ds(parity * rows, rows)] = own_ref[:, source, :] + far_ref[:, source, :]
            o_ref[pl.ds((1 - parity) * rows, rows)] = near_ref[:, source, :] + diag_ref[:, source, :]
            o_ref[2 * rows] = meta.astype(BF)
    if own_only:
        o_ref, low_ref, up_ref, gap_ref = o_refs
        source = Source(o_ref, 0, patch, 4 * rows, SKEW)
        source.gaps(gap_ref)
        tighten(source, gap_ref, range(2 * patch, 3 * patch - 1), low_ref)
        tighten(source, gap_ref, range(1, patch), up_ref)


def merge_rows(ids, centres, share, patch, own_only, *packs):
    rows, half, cells = packs[0][0].shape
    units = [2 * rows + 1, rows // 2 + 1, rows // 2 + 1] if own_only else [2 * rows + 1] * (len(packs) * half // share)
    return pl.pallas_call(
        functools.partial(merge_kernel, chips=len(packs), own_only=own_only, patch=patch),
        in_specs=[pl.BlockSpec(memory_space=pltpu.SMEM)] + [pl.BlockSpec(memory_space=pltpu.VMEM)] * (1 + 4 * len(packs)),
        out_specs=[pl.BlockSpec(memory_space=pltpu.VMEM)] * len(units),
        out_shape=[jax.ShapeDtypeStruct((n, share, cells), BF) for n in units],
        scratch_shapes=[pltpu.VMEM((2, 2 * rows, share, cells), BF)] if own_only else [],
        compiler_params=pltpu.CompilerParams(vmem_limit_bytes=16 * 2**20),
    )(ids, centres, *(array for pack in packs for array in pack))


class Source:
    def __init__(self, ref, hop, patch, total_rows, step=STEP):
        self.ref, self.hop, self.patch, self.total_rows, self.step = ref, hop, patch, total_rows, step
        self.slots = total_rows // 2
        units, self.share, self.cells = ref.shape
        meta = ref[units - 1].astype(F32)
        shape = (self.share, self.cells)
        self.first, self.second, self.third = (jnp.broadcast_to(meta[:, c : c + 1], shape) for c in range(3))
        self.start = iota(shape, 1) - self.third.astype(I32) + self.cells // 2

    def off(self, p):
        place = self.step * (p + self.patch * self.hop)
        return (jnp.bitwise_and(self.start - place, self.cells - 1) - self.cells // 2).astype(F32)

    def limit(self, p):
        off_z, off_x = self.off(p), float(p - self.patch) - self.first
        radius = 3 * self.patch // 2
        return float(radius * radius) - off_x * off_x - off_z * off_z

    def limits(self, plane_sets, out_ref):
        every = {p: self.limit(p) for p in sorted(set().union(*plane_sets))}
        for n, planes in enumerate(plane_sets):
            for odd in range(2):
                value = jnp.full((self.share, self.cells), -1.0, F32)
                for p in planes:
                    if p % 2 == odd:
                        value = jnp.maximum(value, every[p])
                out_ref[n, odd] = value.astype(BF)

    def gaps(self, gap_ref):
        row = self.second.astype(I32)
        for s in range(self.slots):
            ahead = s - row + self.slots // 2
            off = (jnp.bitwise_and(ahead, self.slots - 1) - self.slots // 2).astype(F32)
            gap_ref[0, s] = (off * off).astype(BF)
            gap_ref[1, s] = (jnp.bitwise_and(ahead, self.total_rows - 1) < self.slots).astype(F32).astype(BF)

    def packed(self, s, part):
        value = self.ref[s, part, :]
        turn = STEP * self.patch * self.hop
        even = pltpu.roll(value, turn % self.cells, 1) if turn % self.cells else value
        return even, pltpu.roll(value, (turn + self.cells // 2) % self.cells, 1)

    def parts(self, size):
        return [slice(c, c + size) for c in range(0, self.share, size)]


def tighten(source, gap_ref, planes, o_ref):
    half = source.slots // 2
    cells = source.cells
    limits = {p: source.limit(p).astype(BF) for p in planes}
    turn = (PAIR_SKEW - SKEW) % cells
    rows = []
    for r in range(half):
        total = None
        for later in range(2):
            s = r + half * later
            value, gap = source.ref[s], gap_ref[0, s]
            some = None
            for p in reversed(planes):
                piece = jnp.where(gap <= limits[p], value, jnp.zeros_like(value))
                some = piece if some is None else piece + pltpu.roll(some, turn, 1)
            total = total + pltpu.roll(some, PAIR_ROW, 1) if later else some
        rows.append(total + pltpu.roll(total, cells // 2, 1))
    lane = iota((source.share, cells), 1)
    for u in range(half // 2):
        o_ref[u] = jnp.where(lane < cells // 2, rows[u], rows[u + half // 2])
    o_ref[half // 2] = source.ref[source.ref.shape[0] - 1]


def loosen_kernel(low_ref, up_ref, low_out_ref, up_out_ref, gap_ref, *, patch, total_rows):
    for ref, o_ref, planes in ((low_ref, low_out_ref, range(2 * patch, 3 * patch - 1)), (up_ref, up_out_ref, range(1, patch))):
        source = Source(ref, 0, patch, total_rows, SKEW)
        source.gaps(gap_ref)
        cells, half = source.cells, source.slots // 2
        limits = {p: source.limit(p).astype(BF) for p in planes}
        lane = iota((source.share, cells), 1)
        for u in range(half // 2):
            value = ref[u]
            turned = pltpu.roll(value, cells // 2, 1)
            for group in range(2):
                both = jnp.where(lane < cells // 2, *((value, turned) if group == 0 else (turned, value)))
                for later in range(2):
                    s = u + half // 2 * group + half * later
                    gap = gap_ref[0, s]
                    total = jnp.zeros_like(value)
                    for p in planes:
                        turn = (SKEW - PAIR_SKEW) * (p - planes[0]) - PAIR_ROW * later
                        total = jnp.where(gap <= limits[p], pltpu.roll(both, turn % cells, 1) if turn else both, total)
                    o_ref[s] = total
        o_ref[source.slots] = ref[half // 2]


def loosen(low, up, patch, total_rows):
    slots = total_rows // 2
    vm = pl.BlockSpec(memory_space=pltpu.VMEM)
    return pl.pallas_call(
        functools.partial(loosen_kernel, patch=patch, total_rows=total_rows),
        in_specs=[vm] * 2,
        out_specs=[vm] * 2,
        out_shape=[jax.ShapeDtypeStruct((slots + 1, *low.shape[1:]), BF)] * 2,
        scratch_shapes=[pltpu.VMEM((2, slots, *low.shape[1:]), BF)],
        compiler_params=pltpu.CompilerParams(vmem_limit_bytes=16 * 2**20),
        cost_estimate=pl.CostEstimate(flops=10**6, bytes_accessed=10**4, transcendentals=0),
    )(low, up)


def inside(gap, limit_ref, n, part, even, odd):
    zero = jnp.zeros_like(even)
    return jnp.where(gap <= limit_ref[n, 0, part, :], even, jnp.where(gap <= limit_ref[n, 1, part, :], odd, zero))


def planes_of(quads, allowed, patch, shift):
    return [[p for p in range(patch * q + shift, patch * (q + 1) + shift) if p in allowed] for q in quads]


def spread_rows(source, limit_ref, gap_ref, quads, store):
    def body(n, carry):
        for part in source.parts(A_PART):
            found = []
            for step in range(A_STEP):
                s = n * A_STEP + step
                even, odd = source.packed(s, part)
                gap = gap_ref[0, s, part, :]
                is_low = gap_ref[1, s, part, :] > 0.5
                zero = jnp.zeros_like(even)
                for n_q, q in enumerate(quads):
                    value = inside(gap, limit_ref, n_q, part, even, odd)
                    found.append((q, s, part, jnp.where(is_low, value, zero)))
                    found.append((q, s + source.slots, part, jnp.where(is_low, zero, value)))
            for item in found:
                store(*item)
        return carry

    lax.fori_loop(0, source.slots // A_STEP, body, 0, unroll=A_UNROLL)


def columns(source, allowed, limit_ref, gap_ref, group_ref, v_ref, store):
    patch, cells, share, slots = source.patch, source.cells, source.share, source.slots
    shift = -patch * source.hop
    quads = sorted({(p - shift) // patch for p in allowed})
    sets = planes_of(quads, allowed, patch, shift) + planes_of(quads, allowed, patch, shift - 1) + planes_of(quads, allowed, patch, shift + 1)
    source.limits(sets, limit_ref)
    source.gaps(gap_ref)
    count = len(quads)
    for n, q in enumerate(quads):
        group = jnp.zeros((share, cells), F32)
        for g in range(1, patch):
            group = jnp.where(jnp.abs(source.off(patch * q + shift + g)) <= float(NEAR), float(g), group)
        group_ref[n] = group

    for part in source.parts(S_PART):

        def look(s, part=part):
            even, odd = source.packed(s, part)
            gap = gap_ref[0, s, part, :]
            return even, odd, [inside(gap, limit_ref, n, part, even, odd) for n in range(count)]

        def wide(values):
            return [value.astype(F32) for value in values]

        def body(s, carry, part=part):
            before, even, odd, now = carry
            next_even, next_odd, after = look(jnp.bitwise_and(s + 1, slots - 1))
            gap = gap_ref[0, s, part, :]
            low = gap_ref[1, s, part, :]
            low_packed = low > 0.5
            low_wide = low.astype(F32) > 0.5
            found = []
            for n, q in enumerate(quads):
                value = now[n]
                below = pltpu.roll(inside(gap, limit_ref, count + n, part, even, odd), STEP, 1)
                above = pltpu.roll(inside(gap, limit_ref, 2 * count + n, part, even, odd), cells - STEP, 1)
                beside = below.astype(F32) + above.astype(F32)
                beside = beside + (before[n].astype(F32) + after[n].astype(F32))
                beside = beside + (pltpu.roll(value, 1, 1).astype(F32) + pltpu.roll(value, cells - 1, 1).astype(F32))
                group = group_ref[n, part, :]
                field = None
                for g in range(patch):
                    row = jnp.where(low_wide, *(v_ref[patch * q + g, pl.ds(y, 1), :] for y in (s, s + slots)))
                    field = row if g == 0 else jnp.where(group == float(g), row, field)
                centre = value.astype(F32)
                applied = (0.5 * (6.0 * centre - beside) + field * centre).astype(BF)
                zero = jnp.zeros_like(value)
                found.append((q, 0, s, part, jnp.where(low_packed, value, zero)))
                found.append((q, 0, s + slots, part, jnp.where(low_packed, zero, value)))
                found.append((q, 1, s, part, jnp.where(low_packed, applied, zero)))
                found.append((q, 1, s + slots, part, jnp.where(low_packed, zero, applied)))
            for item in found:
                store(*item)
            return now, next_even, next_odd, after

        lax.fori_loop(0, slots, body, (look(slots - 1)[2], *look(0)), unroll=S_UNROLL)


def row_of(y, cells):
    return pl.ds(pl.multiple_of(y * cells, cells), cells)


def product_of(b, a):
    return lax.dot_general(b, a, (((1,), (1,)), ((), ())), preferred_element_type=F32)


def own_kernel(ids_ref, own_ref, *rest, patch, total_rows, parts):
    field_refs, (b_ref, v_ref, limit_ref, gap_ref, group_ref) = rest[:parts], rest[parts:]
    m = ids_ref[0]
    share, cells = own_ref.shape[1:]
    rows = total_rows // parts
    for hop, ref in enumerate(field_refs):
        to = pl.ds(pl.multiple_of(jnp.bitwise_xor(m, hop) * rows, rows), rows)
        for p in range(3 * patch):
            v_ref[p, to, :] = pltpu.roll(ref[p], STEP * p % cells, 1) if p else ref[p]

    def store_column(q, applied, y, part, value):
        at = applied * share
        b_ref[q, at + part.start : at + part.stop, row_of(y, cells)] = value

    source = Source(own_ref, 0, patch, total_rows)
    every = range(1, 3 * patch - 1)
    columns(source, every, limit_ref, gap_ref, group_ref, v_ref, store_column)


def rows_kernel(ids_ref, *refs, patch, total_rows, parts):
    row_refs, (a_ref, limit_ref, gap_ref) = refs[:parts], refs[parts:]
    share, cells = row_refs[0].shape[1:]
    every = range(1, 3 * patch - 1)
    for n, ref in enumerate(row_refs):
        who = jnp.bitwise_xor(jnp.bitwise_and(ids_ref[0], 2), n) * share
        source = Source(ref, 0, patch, total_rows)
        source.limits(planes_of(range(3), every, patch, 0), limit_ref)
        source.gaps(gap_ref)

        def store_row(q, y, part, value, who=who):
            size = part.stop - part.start
            a_ref[q, pl.ds(pl.multiple_of(who + part.start, size), size), row_of(y, cells)] = value

        spread_rows(source, limit_ref, gap_ref, range(3), store_row)


def others_kernel(
    ids_ref, pairs_ref, row_third_ref, own_ref, low2_ref, low1_ref, up1_ref, up2_ref, a_ref, v_ref, own_b_ref,
    gram_ref, ham_ref,
    b_ref, limit_ref, gap_ref, group_ref,
    *, patch, total_rows,
):
    m = ids_ref[0]
    slots = total_rows // 2
    share, cells = own_ref.shape[1:]
    both = 2 * share
    window = 3 * patch
    spots = {}
    for hop, ref, allowed in (
        (-1, low1_ref, range(patch, window - 1)),
        (1, up1_ref, range(1, 2 * patch)),
        (-2, low2_ref, range(2 * patch, window - 1)),
        (2, up2_ref, range(1, patch)),
    ):
        def store_column(q, applied, y, part, value, hop=hop):
            taken = sorted({q - 2, q - 1, q} - {0}).index(hop)
            spots[hop, q] = taken
            at = taken * both + applied * share
            b_ref[q, at + part.start : at + part.stop, row_of(y, cells)] = value

        source = Source(ref, hop, patch, total_rows)
        columns(source, allowed, limit_ref, gap_ref, group_ref, v_ref, store_column)

    sums = {}
    for q in range(3):
        product = product_of(jnp.concatenate([b_ref[q], own_b_ref[q]], axis=0), a_ref[q])
        for hop in sorted({q - 2, q - 1, q}):
            taken = spots.get((hop, q), 2)
            piece = product[taken * both : (taken + 1) * both]
            sums[hop] = piece if hop not in sums else sums[hop] + piece

    orbs = a_ref.shape[1]
    half_rows = orbs // pairs_ref.shape[0]
    column_block = (m * share) // half_rows
    row_third = row_third_ref[...]
    row_block = iota((1, orbs), 1) // half_rows
    for k, ref in enumerate((low2_ref, low1_ref, own_ref, up1_ref, up2_ref)):
        column_third = ref[slots].astype(F32)[:, 2:3]
        weight = jnp.zeros((1, orbs), F32)
        for g in range(pairs_ref.shape[0]):
            weight = jnp.where(row_block == g, pairs_ref[g, k, column_block].astype(F32), weight)
        weight = jnp.where(jnp.abs(row_third - column_third) <= float(NEAR), weight, 0.0)
        gram_ref[k] = sums[k - 2][:share] * weight
        ham_ref[k] = sums[k - 2][share:] * weight


def products(ids, pairs, row_third, own, rows, others, fields, patch, total_rows, orbs):
    share, cells = rows[0].shape[1:]
    slots = total_rows // 2
    long = total_rows * cells
    vm = pl.BlockSpec(memory_space=pltpu.VMEM)
    sm = pl.BlockSpec(memory_space=pltpu.SMEM)
    params = pltpu.CompilerParams(vmem_limit_bytes=26 * 2**20)
    cost = pl.CostEstimate(flops=10**6, bytes_accessed=10**4, transcendentals=0)
    sizes = dict(patch=patch, total_rows=total_rows)

    def scratch(quads):
        return [
            pltpu.VMEM((3 * quads, 2, share, cells), BF),
            pltpu.VMEM((2, slots, share, cells), BF),
            pltpu.VMEM((quads, share, cells), F32),
        ]

    b, v = pl.pallas_call(
        functools.partial(own_kernel, **sizes, parts=len(rows)),
        in_specs=[sm] + [vm] * (1 + len(fields)),
        out_specs=[vm] * 2,
        out_shape=[jax.ShapeDtypeStruct((3, 2 * share, long), BF), jax.ShapeDtypeStruct((3 * patch, total_rows, cells), F32)],
        scratch_shapes=scratch(3),
        compiler_params=params,
        cost_estimate=cost,
    )(ids, own, *fields)
    a = pl.pallas_call(
        functools.partial(rows_kernel, **sizes, parts=len(rows)),
        in_specs=[sm] + [vm] * len(rows),
        out_specs=vm,
        out_shape=jax.ShapeDtypeStruct((3, orbs, long), BF),
        scratch_shapes=[pltpu.VMEM((3, 2, share, cells), BF), pltpu.VMEM((2, slots, share, cells), BF)],
        compiler_params=params,
        cost_estimate=cost,
    )(ids, *rows)
    out = jax.ShapeDtypeStruct((5, share, orbs), F32)
    return pl.pallas_call(
        functools.partial(others_kernel, **sizes),
        in_specs=[sm, sm] + [vm] * 9,
        out_specs=[vm, vm],
        out_shape=[out, out],
        scratch_shapes=[pltpu.VMEM((3, 4 * share, long), BF)] + scratch(2),
        compiler_params=params,
        cost_estimate=cost,
    )(ids, pairs, row_third, own, *others, a, v, b)


def hop(x, k):
    return lax.ppermute(x, "mat", [(i, i ^ k) for i in range(lax.axis_size("mat"))])


def along(x, distance):
    size = lax.axis_size("dom")
    return lax.ppermute(x, "dom", [((i - distance) % size, i) for i in range(size)])


def on_device(orbitals, potential, centre_first, centre_second, centre_third, correlation_pairs):
    orbs, window, rows, cells = orbitals.shape
    patch = potential.shape[0]
    parts = lax.axis_size("mat")
    ids = lax.axis_index("mat")[None]

    centres = jnp.stack([centre_first, centre_second, centre_third])
    away = pack(ids, centres, orbitals, parts, patch, 0)
    before, after = along(potential, 1), along(potential, -1)
    away, before, after = lax.optimization_barrier((away, before, after))
    far_home = hop(away, 2)
    home = pack(ids, centres, orbitals, parts, patch, 1)
    far_away = hop(home, 2)
    near_home, near_away = hop(home, 1), hop(away, 1)
    field = jnp.concatenate([before, potential, after], axis=0)
    far_field, near_field = hop(field, 2), hop(field, 1)
    far_home, far_field, near_field, home = lax.optimization_barrier((far_home, far_field, near_field, home))
    diag_home, diag_field = hop(far_home, 1), hop(far_field, 1)
    diag_home, diag_field = lax.optimization_barrier((diag_home, diag_field))
    fields = (field, near_field, far_field, diag_field)
    centres = centres.T.astype(F32)
    share = orbs // parts
    homes = (home, near_home, far_home, diag_home)
    merged, low2, up2 = merge_rows(ids, centres, share, patch, True, homes)
    low2, low1, up1, up2 = along(low2, 2), along(merged, 1), along(merged, -1), along(up2, -2)
    far_away, low2, up2 = lax.optimization_barrier((far_away, low2, up2))
    every = merge_rows(ids, centres, share, patch, False, homes, (away, near_away, far_away, hop(far_away, 1)))
    low2, up2 = loosen(low2, up2, patch, rows * parts)
    others = (low2, low1, up1, up2)
    row_third = centre_third.astype(F32)[None, :]
    return tuple(products(ids, correlation_pairs, row_third, merged, every, others, fields, patch, rows * parts, orbs))


def solution(mesh):
    return jax.shard_map(
        on_device,
        mesh=mesh,
        in_specs=(
            P("dom", None, "mat", None),
            P("dom", "mat", None),
            P("dom"),
            P("dom"),
            P("dom"),
            P("dom", None, None),
        ),
        out_specs=(P(None, "mat", "dom"), P(None, "mat", "dom")),
        check_vma=False,
    )
```
